256 devices in a mesh: pole: 4 (over x), row: 8 (over y, z_hi), col: 8 (over z_lo, core).
Axes of the slice: x: 4, y: 4, z: 8 (z_hi: 2, z_lo: 4; z = z_hi * 4 + z_lo), core: 2. Of those that a mesh axis runs over, the one named last changes fastest.
Arguments:
- root_inverse: float32 [4, 2048, 2048], P('pole', 'row', 'col'), may hold values from -1 to 3
- top_factor: float32 [4, 2, 2048, 1024], P('pole', None, 'row', 'col'), may hold values from -0.125 to 0.125
- parent_factor: float32 [4, 4, 1024, 1024], P('pole', None, 'row', 'col'), may hold values from -0.109375 to 0.109375
- root_factor: float32 [4, 4, 2048, 1024], P('pole', None, 'row', 'col'), may hold values from -0.109375 to 0.109375
- top_pivots_inv: float32 [4, 2, 1024, 1024], P('pole', None, 'row', 'col'), may hold values from -1 to 3
- leaf_pivots_inv: float32 [4, 4, 1024, 1024], P('pole', None, 'row', 'col'), may hold values from -1 to 3
- pattern_top: int32 [2, 16], P(None, 'row'), may hold values 0 or 1
- pattern_parent: int32 [4, 8], P(None, 'row'), may hold values 0 or 1
- pattern_root: int32 [4, 16], P(None, 'row'), may hold values 0 or 1
- pole_weights: float32 [4], P('pole'), may hold values from 0.25 to 1
Outputs:
- density_top_diag: float32 [2, 1024, 1024], P(None, 'row', 'col')
- density_top_root: float32 [2, 2048, 1024], P(None, 'row', 'col')
- density_leaf_diag: float32 [4, 1024, 1024], P(None, 'row', 'col')
- density_leaf_parent: float32 [4, 1024, 1024], P(None, 'row', 'col')
- density_leaf_root: float32 [4, 2048, 1024], P(None, 'row', 'col')
The draws below stay inside these ranges and needn't reach their ends.
All inputs are finite; a program needn't handle non-finite values. No bound on the sum of `pattern_top` or of `pattern_parent` or of `pattern_root` on one device may be relied on, other than what follows from the above.
Results may differ from the reference program's by a relative error of at most 0.00013.
Values sent between devices are 32-bit elements; how exact they have to be, the bound alone decides.
No kernel may reach another device: no remote copies, remote signals or barrier semaphores. Data moves between devices by JAX's collectives and lax.ppermute only.
A program may use at most 64 MiB of HBM per device.

```python
import jax
import jax.numpy as jnp
from jax import lax

ROOT_BLOCKS = 16
PARENT_BLOCKS = 8
POLES = 4
ROOT_WIDTH = 2048
PARENT_WIDTH = 1024
LEAF_WIDTH = 1024


def assemble(raw, diag_values):
    width = raw.shape[-1]
    eye = jnp.eye(width, dtype=jnp.float32)
    scaled = raw * (0.5 / jnp.sqrt(jnp.float32(width)))
    return scaled * (1.0 - eye) + eye * diag_values[..., None, :]


def general_draw(key, shape):
    first, second = jax.random.split(key)
    raw = jax.random.truncated_normal(first, -4.0, 4.0, shape, jnp.float32)
    diag_values = jax.random.uniform(second, shape[:-1], jnp.float32, 0.5, 1.5)
    return assemble(raw, diag_values)


def draw_root_inverse(key, part):
    key = jax.random.fold_in(key, 11)
    return general_draw(key, (POLES, ROOT_WIDTH, ROOT_WIDTH))


def draw_top_pivots_inv(key, part):
    key = jax.random.fold_in(key, 23)
    return general_draw(key, (POLES, 2, PARENT_WIDTH, PARENT_WIDTH))


def draw_leaf_pivots_inv(key, part):
    key = jax.random.fold_in(key, 37)
    return general_draw(key, (POLES, 4, LEAF_WIDTH, LEAF_WIDTH))


def with_ends(drawn, own_key, smallest, largest):
    shape = drawn.shape
    place = [jax.random.randint(jax.random.fold_in(own_key, axis), (), 0, shape[axis]) for axis in range(len(shape))]
    drawn = drawn.at[tuple(place)].set(smallest)
    longest = shape.index(max(shape))
    place[longest] = (place[longest] + 1) % shape[longest]
    return drawn.at[tuple(place)].set(largest)


def level_of(key, extent, cuts, smallest, top_value):
    gain, own = 1.0, jax.random.fold_in(key, 6)
    for axis_at, parts in cuts:
        steps = jnp.exp(jax.random.uniform(jax.random.fold_in(own, axis_at), (parts,), jnp.float32, smallest / len(cuts), top_value / len(cuts)))
        gain = gain * jnp.repeat(steps, extent[axis_at] // parts).reshape([-1 if axis == axis_at else 1 for axis in range(len(extent))])
    return gain


def bell_draw(own_key, shape, scale, limit, cuts=(), kind=jnp.bfloat16):
    result = jax.random.normal(own_key, shape, jnp.float32) * scale
    if len(cuts) > 0:
        result = level_of(own_key, shape, cuts, -0.22, 0.18) * result
    return jnp.clip(result, min=-limit, max=limit).astype(kind)


def setup_inputs(seed: int = 0) -> dict:
    streams_of = jax.random.split(jax.random.key(seed), 11)
    return {
        "root_inverse": draw_root_inverse(jax.random.fold_in(streams_of[10], 71), 0),
        "top_factor": bell_draw(streams_of[1], (POLES, 2, ROOT_WIDTH, PARENT_WIDTH), ROOT_WIDTH ** -0.5, 0.125, ((0, 4), (2, 8), (3, 8)), jnp.float32),
        "parent_factor": bell_draw(streams_of[2], (POLES, 4, PARENT_WIDTH, LEAF_WIDTH), (PARENT_WIDTH + ROOT_WIDTH) ** -0.5, 0.109375, ((0, 4), (2, 8), (3, 8)), jnp.float32),
        "root_factor": bell_draw(streams_of[3], (POLES, 4, ROOT_WIDTH, LEAF_WIDTH), (PARENT_WIDTH + ROOT_WIDTH) ** -0.5, 0.109375, ((0, 4), (2, 8), (3, 8)), jnp.float32),
        "top_pivots_inv": draw_top_pivots_inv(jax.random.fold_in(streams_of[10], 71), 0),
        "leaf_pivots_inv": draw_leaf_pivots_inv(jax.random.fold_in(streams_of[10], 71), 0),
        "pattern_top": with_ends((jax.random.randint(streams_of[6], (2, ROOT_BLOCKS), 0, 4) < 3).astype(jnp.int32), jax.random.fold_in(streams_of[6], 1), 0, 1),
        "pattern_parent": with_ends((jax.random.randint(streams_of[7], (4, PARENT_BLOCKS), 0, 4) < 3).astype(jnp.int32), jax.random.fold_in(streams_of[7], 1), 0, 1),
        "pattern_root": with_ends((jax.random.randint(streams_of[8], (4, ROOT_BLOCKS), 0, 4) < 3).astype(jnp.int32), jax.random.fold_in(streams_of[8], 1), 0, 1),
        "pole_weights": jnp.clip(0.25 + 0.75 * jax.random.uniform(streams_of[9], (POLES,), jnp.float32) ** level_of(streams_of[9], (POLES,), ((0, 4),), -0.2, 0.2), 0.25, 1.0),
    }


def contract(form, left, right):
    return jnp.einsum(form, left, right, precision=lax.Precision.HIGHEST)


def block_mask(pattern, rows):
    width = rows // pattern.shape[-1]
    return jnp.repeat(pattern.astype(jnp.float32), width, axis=-1)


def reference(root_inverse, top_factor, parent_factor, root_factor, top_pivots_inv, leaf_pivots_inv, pattern_top, pattern_parent, pattern_root, pole_weights):
    top_mask = block_mask(pattern_top, top_factor.shape[2])
    parent_mask = block_mask(pattern_parent, parent_factor.shape[2])
    root_mask = block_mask(pattern_root, root_factor.shape[2])
    sums = None
    for index in range(pole_weights.shape[0]):
        inverse = root_inverse[index]
        top_panel = top_factor[index] * top_mask[:, :, None]
        parent_panel = parent_factor[index] * parent_mask[:, :, None]
        root_panel = root_factor[index] * root_mask[:, :, None]
        outer = -contract("ik,ckj->cij", inverse, top_panel)
        top_diag = top_pivots_inv[index] - contract("cki,ckj->cij", outer, top_panel)
        outer_four = jnp.repeat(outer, 2, axis=0)
        diag_four = jnp.repeat(top_diag, 2, axis=0)
        leaf_parent = -(contract("nik,nkj->nij", diag_four, parent_panel) + contract("nki,nkj->nij", outer_four, root_panel))
        leaf_root = -(contract("nik,nkj->nij", outer_four, parent_panel) + contract("ik,nkj->nij", inverse, root_panel))
        leaf_diag = leaf_pivots_inv[index] - (contract("nki,nkj->nij", leaf_parent, parent_panel) + contract("nki,nkj->nij", leaf_root, root_panel))
        weight = pole_weights[index]
        terms = (weight * top_diag, weight * outer, weight * leaf_diag, weight * leaf_parent, weight * leaf_root)
        if sums is None:
            sums = terms
        else:
            sums = tuple(total + term for total, term in zip(sums, terms))
    return (sums[0], sums[1], sums[2], sums[3], sums[4])
```

```python
import jax
import jax.numpy as jnp
from jax import lax
from jax.sharding import Mesh
from jax.sharding import PartitionSpec as P

RING = ("zh", "zl")
LANE = ("zh", "zl", "core")
PLANE = ("y", "zh", "zl", "core")
SIZE_X, SIZE_Y, SIZE_H, SIZE_L, SIZE_C = 4, 4, 2, 4, 2


def mm(form, left, right):
    return jnp.einsum(form, left, right, precision=lax.Precision.HIGH)


def block_mask(pattern, rows):
    width = rows // pattern.shape[-1]
    return jnp.repeat(pattern.astype(jnp.float32), width, axis=-1)


def lane_pairs(target):
    pairs = []
    for zh in range(SIZE_H):
        for zl in range(SIZE_L):
            for core in range(SIZE_C):
                to_h, to_l, to_c = target(zh, zl, core)
                pairs.append(
                    ((zh * SIZE_L + zl) * SIZE_C + core, (to_h * SIZE_L + to_l) * SIZE_C + to_c)
                )
    return pairs


def plane_pairs(flip):
    pairs = []
    for y in range(SIZE_Y):
        for zh in range(SIZE_H):
            for zl in range(SIZE_L):
                for core in range(SIZE_C):
                    here = ((y * SIZE_H + zh) * SIZE_L + zl) * SIZE_C + core
                    there = ((zl * SIZE_H + zh) * SIZE_L + y) * SIZE_C + (core ^ flip)
                    pairs.append((here, there))
    return pairs


def spread(value, axis, size):
    return lax.all_to_all(jnp.broadcast_to(value[None], (size,) + value.shape), axis, 0, 0)


def in_order(flag, first, second):
    return jnp.where(flag == 0, first, second), jnp.where(flag == 0, second, first)


def body(
    root_inverse,
    top_factor,
    parent_factor,
    root_factor,
    top_pivots_inv,
    leaf_pivots_inv,
    pattern_top,
    pattern_parent,
    pattern_root,
    pole_weights,
):
    zh = lax.axis_index("zh")
    zl = lax.axis_index("zl")
    core = lax.axis_index("core")
    weight = pole_weights[0]

    top = top_factor[0] * block_mask(pattern_top, 256)[:, :, None]
    parent = parent_factor[0] * block_mask(pattern_parent, 128)[:, :, None]
    root = root_factor[0] * block_mask(pattern_root, 256)[:, :, None]

    def ring_rows(value):
        return lax.all_gather(value, LANE, axis=0)

    def own(gathered, count):
        shape = gathered.shape
        split = gathered.reshape((shape[0], SIZE_C, count) + shape[2:])
        return lax.dynamic_index_in_dim(split, core, 1, keepdims=False)

    def flat_rows(lanes):
        _, n, rows, cols = lanes.shape
        grid = lanes.reshape(SIZE_H, SIZE_L, SIZE_C, n, rows, cols)
        grid = jnp.transpose(grid, (3, 0, 4, 1, 2, 5))
        return grid.reshape(n, SIZE_H * rows, SIZE_L * SIZE_C * cols)

    inverse_rows = flat_rows(ring_rows(root_inverse))[0]
    inverse_rows = inverse_rows.reshape(512, 2048)
    top_rows = flat_rows(own(ring_rows(top), 1))[0]
    pivot_rows = flat_rows(own(ring_rows(top_pivots_inv[0]), 1))[0]
    parent_rows = flat_rows(own(ring_rows(parent), 2))
    root_rows = flat_rows(own(ring_rows(root), 2))

    panels = jnp.concatenate(
        [
            top,
            parent.reshape(2, 256, 128),
            root.reshape(2, 512, 128),
        ],
        axis=1,
    )
    got = []
    for flip in range(2):
        piece = lax.dynamic_index_in_dim(panels, zh ^ flip, 0, keepdims=False)
        got.append(
            lax.ppermute(piece, LANE, lane_pairs(lambda h, l, c: (c, l, h ^ flip)))
        )
    low, high = in_order(core, got[0], got[1])
    top_block = jnp.concatenate([low[:256], high[:256]], axis=0)
    parent_block = jnp.stack(
        [low[256:512].reshape(2, 128, 128), high[256:512].reshape(2, 128, 128)], axis=1
    ).reshape(2, 256, 128)
    root_block = jnp.stack(
        [low[512:].reshape(2, 256, 128), high[512:].reshape(2, 256, 128)], axis=1
    ).reshape(2, 512, 128)

    top_cols = spread(top_block, "y", SIZE_Y).reshape(2048, 128)
    parent_cols = jnp.moveaxis(spread(parent_block, "y", SIZE_Y), 1, 0).reshape(2, 1024, 128)

    outer = -mm("ik,kj->ij", inverse_rows, top_cols)
    turned = lax.ppermute(outer, PLANE, plane_pairs(0))
    turned = lax.all_gather(turned, RING, axis=0)
    outer_turned = jnp.transpose(
        turned.reshape(SIZE_H, SIZE_L, 512, 128), (1, 2, 0, 3)
    ).reshape(2048, 256)

    rest = root_block - mm("ik,nkj->nij", top_rows, parent_cols)
    rest_cols = jnp.moveaxis(spread(rest, "y", SIZE_Y), 1, 0).reshape(2, 2048, 128)
    leaf_root = -mm("ik,nkj->nij", inverse_rows, rest_cols)

    pivot_block = lax.dynamic_slice_in_dim(pivot_rows, (zl * SIZE_H + zh) * 128, 128, 1)
    top_diag = pivot_block - mm("ki,kj->ij", outer_turned, top_cols)
    leaf_parent = -(
        mm("ik,nkj->nij", pivot_rows, parent_cols) + mm("ki,nkj->nij", outer_turned, rest_cols)
    )

    def by_half(value):
        return value.reshape(value.shape[:-2] + (SIZE_H, value.shape[-2] // SIZE_H, 128))

    blocks = weight * jnp.concatenate(
        [
            by_half(top_diag),
            by_half(outer),
            by_half(leaf_parent[0]),
            by_half(leaf_parent[1]),
            by_half(leaf_root[0]),
            by_half(leaf_root[1]),
        ],
        axis=1,
    )
    blocks = jnp.moveaxis(blocks.reshape(SIZE_H, SIZE_X, 288, 128), 1, 0)
    summed = jnp.sum(lax.all_to_all(blocks, "pole", 0, 0), axis=0)
    got = []
    for flip in range(2):
        piece = lax.dynamic_index_in_dim(summed, core ^ flip, 0, keepdims=False)
        got.append(
            lax.ppermute(piece, LANE, lane_pairs(lambda h, l, c: (c ^ flip, l, h)))
        )
    pair = jnp.stack(in_order(zh, got[0], got[1]), axis=0)
    every = spread(pair, "pole", SIZE_X)
    every = jnp.moveaxis(every, 0, 1).reshape(2, 1152, 128)
    top_dens = every[:, :128]
    outer_dens = every[:, 128:384]
    parent_dens = every[:, 384:640].reshape(4, 128, 128)
    rootward_dens = every[:, 640:].reshape(4, 256, 128)

    cross = mm("nki,nkj->nij", leaf_parent, parent_rows) + mm(
        "nki,nkj->nij", leaf_root, root_rows
    )
    cross = (weight * cross).reshape(2, SIZE_X, 32, SIZE_Y, 256)
    cross = jnp.transpose(cross, (1, 3, 0, 2, 4)).reshape(16, 2, 32, 256)
    cross = jnp.sum(lax.all_to_all(cross, ("pole", "y"), 0, 0), axis=0)
    got = []
    halves = cross.reshape(2, 32, 2, 128)
    for flip in range(2):
        piece = lax.dynamic_index_in_dim(halves, core ^ flip, 2, keepdims=False)
        got.append(lax.ppermute(piece, PLANE, plane_pairs(flip)))
    cross = jnp.concatenate(in_order(core, got[0], got[1]), axis=0)

    leaf = (weight * leaf_pivots_inv[0]).reshape(4, SIZE_X, 32, 128)
    leaf = jnp.sum(lax.all_to_all(jnp.moveaxis(leaf, 1, 0), "pole", 0, 0), axis=0)
    leaf_dens = jnp.moveaxis(spread(leaf - cross, "pole", SIZE_X), 0, 1).reshape(4, 128, 128)
    return (top_dens, outer_dens, leaf_dens, parent_dens, rootward_dens)


def solution(mesh):
    fine = Mesh(
        mesh.devices.reshape(SIZE_X, SIZE_Y, SIZE_H, SIZE_L, SIZE_C),
        ("pole", "y", "zh", "zl", "core"),
    )
    row, col = ("y", "zh"), ("zl", "core")
    return jax.shard_map(
        body,
        mesh=fine,
        in_specs=(
            P("pole", row, col),
            P("pole", None, row, col),
            P("pole", None, row, col),
            P("pole", None, row, col),
            P("pole", None, row, col),
            P("pole", None, row, col),
            P(None, row),
            P(None, row),
            P(None, row),
            P("pole"),
        ),
        out_specs=(
            P(None, row, col),
            P(None, row, col),
            P(None, row, col),
            P(None, row, col),
            P(None, row, col),
        ),
        check_vma=False,
    )
```

```python
import math

import jax
import jax.numpy as jnp
from jax import lax
from jax.experimental import pallas as pl
from jax.experimental.pallas import tpu as pltpu
from jax.sharding import Mesh
from jax.sharding import PartitionSpec as P

RING = ("zh", "zl")
LANE = ("zh", "zl", "core")
PLANE = ("y", "zh", "zl", "core")
SIZE_X, SIZE_Y, SIZE_H, SIZE_L, SIZE_C = 4, 4, 2, 4, 2
SIZE_Z = SIZE_H * SIZE_L
VMEM = pltpu.CompilerParams(vmem_limit_bytes=64 * 1024 * 1024)
IN_VMEM = pl.BlockSpec(memory_space=pltpu.VMEM)
IN_SMEM = pl.BlockSpec(memory_space=pltpu.SMEM)


def block_mask(pattern, rows):
    width = rows // pattern.shape[-1]
    return jnp.repeat(pattern.astype(jnp.float32), width, axis=-1)


def lane_pairs(target):
    pairs = []
    for zh in range(SIZE_H):
        for zl in range(SIZE_L):
            for core in range(SIZE_C):
                to_h, to_l, to_c = target(zh, zl, core)
                pairs.append(
                    ((zh * SIZE_L + zl) * SIZE_C + core, (to_h * SIZE_L + to_l) * SIZE_C + to_c)
                )
    return pairs


def plane_pairs(flip):
    pairs = []
    for y in range(SIZE_Y):
        for zh in range(SIZE_H):
            for zl in range(SIZE_L):
                for core in range(SIZE_C):
                    here = ((y * SIZE_H + zh) * SIZE_L + zl) * SIZE_C + core
                    there = ((zl * SIZE_H + zh) * SIZE_L + y) * SIZE_C + (core ^ flip)
                    pairs.append((here, there))
    return pairs


def ring_pairs(step):
    return [(z, (z + step) % SIZE_Z) for z in range(SIZE_Z)]


def onward(pieces, step):
    ahead, behind = (pieces[-2], pieces[-1]) if step else (pieces[0], pieces[0])
    if step == 3:
        half = ahead.shape[0] // 2
        ahead, behind = ahead[:half], behind[half:]
    return [
        lax.ppermute(ahead, RING, ring_pairs(1)),
        lax.ppermute(behind, RING, ring_pairs(-1)),
    ]


def column_of(place):
    return (place % SIZE_L) * SIZE_H + place // SIZE_L


def spread(value, axis, size):
    return lax.all_to_all(jnp.broadcast_to(value[None], (size,) + value.shape), axis, 0, 0)


def in_order(flag, first, second):
    return jnp.where(flag == 0, first, second), jnp.where(flag == 0, second, first)


def split(value):
    high = value.astype(jnp.bfloat16)
    return high, (value - high.astype(jnp.float32)).astype(jnp.bfloat16)


def product(left, right, dims=((1,), (0,))):
    def one(a, b):
        return lax.dot_general(a, b, (dims, ((), ())), preferred_element_type=jnp.float32)

    return one(left[0], right[0]) + (one(left[0], right[1]) + one(left[1], right[0]))


def product_t(left, right):
    return product(left, right, ((0,), (0,)))


def fetched(sources, scratch, sems):
    copies = [
        pltpu.make_async_copy(source, to, sems.at[at])
        for at, (source, to) in enumerate(zip(sources, scratch))
    ]
    for copy in copies:
        copy.start()

    def ready(at):
        copies[at].wait()
        return scratch[at]

    return ready


def outer_kernel(inverse, top, out, inverse_here, top_here, sems):
    order = [half * 8 + k for k in range(8) for half in range(2)]
    ready = fetched(
        [top.at[:, 0:256, :]] + [inverse.at[at] for at in order],
        [top_here.at[:, 0:256, :]] + [inverse_here.at[at] for at in order],
        sems,
    )
    ready(0)
    totals = [None, None]
    for k in range(8):
        right = split(top_here[k, 0:256, :])
        for half in range(2):
            left = split(ready(1 + k * 2 + half)[...])
            part = product(left, right)
            totals[half] = part if k == 0 else totals[half] + part
    for half in range(2):
        out[half * 256 : (half + 1) * 256, :] = -totals[half]


def cross_kernel(order, *refs):
    sources, (top_out, leaf_out) = refs[:10], refs[10:12]
    scratch, sems = refs[12:22], refs[22]
    ready = fetched(sources, scratch, sems)
    mine = ready(0)
    panels = split(
        jnp.concatenate(
            [
                jnp.concatenate(
                    [mine[zh, 0:256, :], mine[zh, 512:768, :], mine[zh, 768:1024, :]], axis=1
                )
                for zh in range(SIZE_H)
            ],
            axis=0,
        )
    )
    for at in range(8):
        if at < 7:
            piece = ready(1 + at)[...]
        else:
            piece = jnp.concatenate([ready(8)[...], ready(9)[...]], axis=0)
        part = product_t(split(piece), panels)
        top_out[order[at]] = part[:, :128]
        leaf_out[order[at], 0] = part[:, 128:256]
        leaf_out[order[at], 1] = part[:, 256:]


def root_kernel(order, *refs):
    sources, out = refs[:12], refs[12]
    scratch, sems = refs[13:25], refs[25]
    ready = fetched(sources, scratch, sems)
    cols, last, inverse = ready(0), ready(1), ready(2)
    totals = [jnp.zeros((256, 256), jnp.float32) for _ in range(2)]
    for k in range(8):
        root = split(jnp.concatenate([cols[k, 512:768, :], last[k]], axis=1))
        for half in range(2):
            totals[half] += product(split(inverse[half * 8 + k]), root)
    for at in range(8):
        if at < 7:
            piece = ready(3 + at)[...]
        else:
            piece = jnp.concatenate([ready(10)[...], ready(11)[...]], axis=0)
        place = order[at]
        parent = split(
            jnp.concatenate([cols[place, 256:384, :], cols[place, 384:512, :]], axis=1)
        )
        for half in range(2):
            totals[half] += product(split(piece[half * 256 : (half + 1) * 256]), parent)
    for half in range(2):
        for leaf in range(2):
            out[leaf, half * 256 : (half + 1) * 256, :] = -totals[half][
                :, leaf * 128 : (leaf + 1) * 128
            ]


def parent_kernel(order, *refs):
    sources, out, scratch, sems = refs[:11], refs[11], refs[12:23], refs[23]
    ready = fetched(sources, scratch, sems)
    cols, cross = ready(0), ready(1)
    total = jnp.zeros((256, 256), jnp.float32)
    for at in range(8):
        if at < 7:
            piece = ready(2 + at)[...]
        else:
            piece = jnp.concatenate([ready(9)[...], ready(10)[...]], axis=0)
        place = order[at]
        parent = jnp.concatenate([cols[place, 256:384, :], cols[place, 384:512, :]], axis=1)
        total += product(split(piece), split(parent))
    for leaf in range(2):
        for sub in range(2):
            added = cross[0, sub, leaf]
            for y in range(1, SIZE_Y):
                added += cross[y, sub, leaf]
            rows = slice(sub * 128, (sub + 1) * 128)
            out[leaf, rows, :] = -(total[rows, leaf * 128 : (leaf + 1) * 128] + added)


def leaf_kernel(core, weight, parent, root, panels, out, total, high, low):
    block, half = pl.program_id(0), pl.program_id(1)

    @pl.when(block == 0)
    def _():
        for leaf in range(2):
            rows = jnp.concatenate([parent[leaf], root[leaf]], axis=0)
            high[half, leaf], low[half, leaf] = split(jnp.transpose(rows))

    for leaf in range(2):
        right = split(jnp.concatenate([panels[0, leaf], panels[1, leaf]], axis=1))
        part = product((high[half, leaf], low[half, leaf]), right)

        @pl.when(half == 0)
        def _():
            total[leaf] = part

        @pl.when(half == 1)
        def _():
            done = weight[0] * (total[leaf] + part)
            for side in range(2):
                out[:, 0, side, leaf] = done[:, side * 128 : (side + 1) * 128].reshape(
                    SIZE_X, 32, 128
                )


def leaf_cross(core, weight, parent, root, panels):
    return pl.pallas_call(
        leaf_kernel,
        out_shape=jax.ShapeDtypeStruct((SIZE_X, SIZE_Y, 2, 2, 32, 128), jnp.float32),
        grid_spec=pltpu.PrefetchScalarGridSpec(
            num_scalar_prefetch=1,
            grid=(SIZE_L, SIZE_H),
            in_specs=[
                IN_SMEM,
                pl.BlockSpec((2, 128, 128), lambda l, h, core: (0, h, 0)),
                pl.BlockSpec((2, 256, 128), lambda l, h, core: (0, h, 0)),
                pl.BlockSpec((2, 2, 384, 128), lambda l, h, core: (h * 4 + l, core[0], 0, 0)),
            ],
            out_specs=pl.BlockSpec(
                (SIZE_X, 1, 2, 2, 32, 128), lambda l, h, core: (0, l, 0, 0, 0, 0)
            ),
            scratch_shapes=[
                pltpu.VMEM((2, 128, 256), jnp.float32),
                pltpu.VMEM((2, 2, 128, 384), jnp.bfloat16),
                pltpu.VMEM((2, 2, 128, 384), jnp.bfloat16),
            ],
        ),
        cost_estimate=cost(2 * 768 * 1024 * 128, [(2, 768, 1024), (2, 768, 128), (2, 1024, 128)]),
        compiler_params=VMEM,
    )(core, weight, parent, root, panels)


def cost(terms, arrays):
    moved = 4 * sum(math.prod(shape) for shape in arrays)
    return pl.CostEstimate(flops=6 * terms, bytes_accessed=moved, transcendentals=0)


def with_copies(kernel, shapes, order, *operands, terms, copies=None):
    specs = [pl.BlockSpec(memory_space=pl.ANY)] * len(operands)
    scratch = [pltpu.VMEM(operand.shape, jnp.float32) for operand in operands]
    scratch.append(pltpu.SemaphoreType.DMA((copies or len(operands),)))
    price = cost(terms, [operand.shape for operand in operands] + shapes)
    if order is not None:
        specs, operands = [IN_SMEM] + specs, (order,) + operands
    return pl.pallas_call(
        kernel,
        out_shape=[jax.ShapeDtypeStruct(shape, jnp.float32) for shape in shapes],
        in_specs=specs,
        out_specs=[IN_VMEM] * len(shapes),
        scratch_shapes=scratch,
        cost_estimate=price,
        compiler_params=VMEM,
    )(*operands)


def body(
    root_inverse,
    top_factor,
    parent_factor,
    root_factor,
    top_pivots_inv,
    leaf_pivots_inv,
    pattern_top,
    pattern_parent,
    pattern_root,
    pole_weights,
):
    zh = lax.axis_index("zh")
    zl = lax.axis_index("zl")
    core = lax.axis_index("core")
    place = zh * SIZE_L + zl
    weight = pole_weights[0]

    top = top_factor[0] * block_mask(pattern_top, 256)[:, :, None]
    parent = parent_factor[0] * block_mask(pattern_parent, 128)[:, :, None]
    root = root_factor[0] * block_mask(pattern_root, 256)[:, :, None]

    leaves = jnp.concatenate([parent, root], axis=1)

    def to_ring(value):
        got = []
        for flip in range(2):
            piece = lax.dynamic_index_in_dim(value, zh ^ flip, 0, keepdims=False)
            got.append(
                lax.ppermute(piece, LANE, lane_pairs(lambda h, l, c: (c, l, h ^ flip)))
            )
        return jnp.stack(in_order(core, got[0], got[1]))

    block = to_ring(
        jnp.concatenate(
            [top, parent.reshape(2, 256, 128), root.reshape(2, 512, 128), top_pivots_inv[0]],
            axis=1,
        )
    )
    pivot_block = block[:, 1024:].reshape(256, 128)
    first_cols = spread(block[:, :768], "y", SIZE_Y).reshape(8, 768, 128)
    inverse, block = lax.optimization_barrier((root_inverse[0], block))
    inverse = lax.all_gather(inverse, LANE, axis=0)

    leaf = (weight * leaf_pivots_inv[0]).reshape(4, SIZE_X, 32, 128)
    leaf = jnp.sum(lax.all_to_all(jnp.moveaxis(leaf, 1, 0), "pole", 0, 0), axis=0)
    first_cols, leaf = lax.optimization_barrier((first_cols, leaf))

    (outer,) = with_copies(
        outer_kernel,
        [(512, 128)],
        None,
        inverse,
        first_cols,
        terms=512 * 2048 * 128,
        copies=17,
    )
    last_cols = spread(block[:, 768:1024], "y", SIZE_Y).reshape(8, 256, 128)
    pieces = [outer]
    for step in range(3):
        pieces += onward(pieces, step)
    pieces[5], pieces[6], leaves, last_cols = lax.optimization_barrier(
        (pieces[5], pieces[6], leaves, last_cols)
    )
    pieces += onward(pieces, 3)
    panels = lax.all_gather(leaves, LANE, axis=0)
    order = jnp.stack([column_of((place + d) % SIZE_Z) for d in (0, 7, 1, 6, 2, 5, 3, 4)])

    cross_top, cross_leaf = with_copies(
        cross_kernel,
        [(8, 128, 128), (8, 2, 128, 128)],
        order,
        block,
        *pieces,
        terms=512 * 1024 * 384,
    )
    cross_leaf, last_cols = lax.optimization_barrier((cross_leaf, last_cols))
    (leaf_root,) = with_copies(
        root_kernel,
        [(2, 512, 128)],
        order,
        first_cols,
        last_cols,
        inverse,
        *pieces,
        terms=512 * 3072 * 256,
    )
    cross_top = lax.all_to_all(cross_top.reshape(SIZE_Y, 256, 128), "y", 0, 0)
    cross_top, cross_leaf, leaf_root = lax.optimization_barrier(
        (cross_top, cross_leaf, leaf_root)
    )
    cross_leaf = lax.all_to_all(cross_leaf.reshape(SIZE_Y, 2, 2, 128, 128), "y", 0, 0)
    top_diag = pivot_block - jnp.sum(cross_top, axis=0)
    def summed(values):
        blocks = jnp.concatenate(
            [value.reshape(SIZE_H, value.shape[0] // SIZE_H, 128) for value in values], axis=1
        )
        blocks = (weight * blocks).reshape(SIZE_H, SIZE_X, blocks.shape[1] // SIZE_X, 128)
        return jnp.sum(lax.all_to_all(jnp.moveaxis(blocks, 1, 0), "pole", 0, 0), axis=0)

    def in_place(blocks):
        got = []
        for flip in range(2):
            piece = lax.dynamic_index_in_dim(blocks, core ^ flip, 0, keepdims=False)
            got.append(
                lax.ppermute(piece, LANE, lane_pairs(lambda h, l, c: (c ^ flip, l, h)))
            )
        return jnp.stack(in_order(zh, got[0], got[1]), axis=0)

    def everywhere(pair):
        every = jnp.moveaxis(spread(pair, "pole", SIZE_X), 0, 1)
        return every.reshape(pair.shape[0], SIZE_X * pair.shape[1], 128)

    diag_pieces = [top_diag]
    for step in range(3):
        diag_pieces += onward(diag_pieces, step)
    early = summed([outer, leaf_root[0], leaf_root[1]])
    diag_pieces[5], diag_pieces[6], early = lax.optimization_barrier(
        (diag_pieces[5], diag_pieces[6], early)
    )
    diag_pieces += onward(diag_pieces, 3)
    early = in_place(early)
    diag_pieces[7], diag_pieces[8], early = lax.optimization_barrier(
        (diag_pieces[7], diag_pieces[8], early)
    )
    (leaf_parent,) = with_copies(
        parent_kernel,
        [(2, 256, 128)],
        order,
        first_cols,
        cross_leaf,
        *diag_pieces,
        terms=256 * 1024 * 256,
    )
    early = everywhere(early)
    late = summed([top_diag, leaf_parent[0], leaf_parent[1]])

    cross = leaf_cross(core.reshape(1), pole_weights, leaf_parent, leaf_root, panels)
    cross, early = lax.optimization_barrier((cross, early))
    cross = cross.reshape(SIZE_X * SIZE_Y, 2, 2, 32, 128)
    cross = jnp.sum(lax.all_to_all(cross, ("pole", "y"), 0, 0), axis=0)
    late = in_place(late)
    got = []
    for flip in range(2):
        piece = lax.dynamic_index_in_dim(cross, core ^ flip, 0, keepdims=False)
        got.append(lax.ppermute(piece, PLANE, plane_pairs(flip)))
    cross = jnp.concatenate(in_order(core, got[0], got[1]), axis=0)
    ends = everywhere(jnp.concatenate([late.reshape(6, 32, 128), leaf - cross], axis=0))
    outer_dens = early[:, :256]
    rootward_dens = early[:, 256:].reshape(4, 256, 128)
    leaf_dens = ends[6:]
    late = jnp.moveaxis(ends[:6].reshape(2, 3, SIZE_X, 32, 128), 2, 1).reshape(2, 384, 128)
    top_dens = late[:, :128]
    parent_dens = late[:, 128:].reshape(4, 128, 128)
    return (top_dens, outer_dens, leaf_dens, parent_dens, rootward_dens)


def solution(mesh):
    fine = Mesh(
        mesh.devices.reshape(SIZE_X, SIZE_Y, SIZE_H, SIZE_L, SIZE_C),
        ("pole", "y", "zh", "zl", "core"),
    )
    row, col = ("y", "zh"), ("zl", "core")
    return jax.shard_map(
        body,
        mesh=fine,
        in_specs=(
            P("pole", row, col),
            P("pole", None, row, col),
            P("pole", None, row, col),
            P("pole", None, row, col),
            P("pole", None, row, col),
            P("pole", None, row, col),
            P(None, row),
            P(None, row),
            P(None, row),
            P("pole"),
        ),
        out_specs=(
            P(None, row, col),
            P(None, row, col),
            P(None, row, col),
            P(None, row, col),
            P(None, row, col),
        ),
        check_vma=False,
    )
```

```python
import math

import jax
import jax.numpy as jnp
from jax import lax
from jax.experimental import pallas as pl
from jax.experimental.pallas import tpu as pltpu
from jax.sharding import Mesh
from jax.sharding import PartitionSpec as P

RING = ("zh", "zl")
LANE = ("zh", "zl", "core")
PLANE = ("y", "zh", "zl", "core")
SIZE_X, SIZE_Y, SIZE_H, SIZE_L, SIZE_C = 4, 4, 2, 4, 2
SIZE_Z = SIZE_H * SIZE_L
VMEM = pltpu.CompilerParams(vmem_limit_bytes=64 * 1024 * 1024)
IN_VMEM = pl.BlockSpec(memory_space=pltpu.VMEM)
IN_SMEM = pl.BlockSpec(memory_space=pltpu.SMEM)


def block_mask(pattern, rows):
    width = rows // pattern.shape[-1]
    return jnp.repeat(pattern.astype(jnp.float32), width, axis=-1)


def lane_pairs(target):
    pairs = []
    for zh in range(SIZE_H):
        for zl in range(SIZE_L):
            for core in range(SIZE_C):
                to_h, to_l, to_c = target(zh, zl, core)
                pairs.append(
                    ((zh * SIZE_L + zl) * SIZE_C + core, (to_h * SIZE_L + to_l) * SIZE_C + to_c)
                )
    return pairs


def plane_pairs(flip):
    pairs = []
    for y in range(SIZE_Y):
        for zh in range(SIZE_H):
            for zl in range(SIZE_L):
                for core in range(SIZE_C):
                    here = ((y * SIZE_H + zh) * SIZE_L + zl) * SIZE_C + core
                    there = ((zl * SIZE_H + zh) * SIZE_L + y) * SIZE_C + (core ^ flip)
                    pairs.append((here, there))
    return pairs


def ring_pairs(step):
    return [(z, (z + step) % SIZE_Z) for z in range(SIZE_Z)]


def onward(pieces, step):
    ahead, behind = (pieces[-2], pieces[-1]) if step else (pieces[0], pieces[0])
    if step == 3:
        half = ahead.shape[0] // 2
        ahead, behind = ahead[:half], behind[half:]
    return [
        lax.ppermute(ahead, RING, ring_pairs(1)),
        lax.ppermute(behind, RING, ring_pairs(-1)),
    ]


def column_of(place):
    return (place % SIZE_L) * SIZE_H + place // SIZE_L


def spread(value, axis, size):
    return lax.all_to_all(jnp.broadcast_to(value[None], (size,) + value.shape), axis, 0, 0)


def in_order(flag, first, second):
    return jnp.where(flag == 0, first, second), jnp.where(flag == 0, second, first)


def split(value):
    high = value.astype(jnp.bfloat16)
    return high, (value - high.astype(jnp.float32)).astype(jnp.bfloat16)


def product(left, right, dims=((1,), (0,))):
    def one(a, b):
        return lax.dot_general(a, b, (dims, ((), ())), preferred_element_type=jnp.float32)

    return one(left[0], right[0]) + (one(left[0], right[1]) + one(left[1], right[0]))


def product_t(left, right):
    return product(left, right, ((0,), (0,)))


def fetched(sources, scratch, sems):
    copies = [
        pltpu.make_async_copy(source, to, sems.at[at])
        for at, (source, to) in enumerate(zip(sources, scratch))
    ]
    for copy in copies:
        copy.start()

    def ready(at):
        copies[at].wait()
        return scratch[at]

    return ready


def outer_kernel(inverse, top, out, inverse_here, top_here, sems):
    order = [half * 8 + k for k in range(8) for half in range(2)]
    ready = fetched(
        [top] + [inverse.at[at] for at in order],
        [top_here] + [inverse_here.at[at] for at in order],
        sems,
    )
    ready(0)
    totals = [None, None]
    for k in range(8):
        right = split(top_here[k])
        for half in range(2):
            left = split(ready(1 + k * 2 + half)[...])
            part = product(left, right)
            totals[half] = part if k == 0 else totals[half] + part
    for half in range(2):
        out[half * 256 : (half + 1) * 256, :] = -totals[half]


def cross_kernel(order, *refs):
    sources, (top_out, leaf_out) = refs[:11], refs[11:13]
    scratch, sems = refs[13:24], refs[24]
    ready = fetched(sources, scratch, sems)
    top, mine = ready(0), ready(1)
    panels = split(
        jnp.concatenate(
            [
                jnp.concatenate([top[zh], mine[zh, 256:512, :], mine[zh, 512:768, :]], axis=1)
                for zh in range(SIZE_H)
            ],
            axis=0,
        )
    )
    for at in range(8):
        if at < 7:
            piece = ready(2 + at)[...]
        else:
            piece = jnp.concatenate([ready(9)[...], ready(10)[...]], axis=0)
        part = product_t(split(piece), panels)
        top_out[order[at]] = part[:, :128]
        leaf_out[order[at], 0] = part[:, 128:256]
        leaf_out[order[at], 1] = part[:, 256:]


def root_kernel(order, *refs):
    sources, out = refs[:11], refs[11]
    scratch, sems = refs[12:23], refs[23]
    ready = fetched(sources, scratch, sems)
    cols, inverse = ready(0), ready(1)
    totals = [jnp.zeros((256, 256), jnp.float32) for _ in range(2)]
    for k in range(8):
        root = split(jnp.concatenate([cols[k, 256:512, :], cols[k, 512:768, :]], axis=1))
        for half in range(2):
            totals[half] += product(split(inverse[half * 8 + k]), root)
    for at in range(8):
        if at < 7:
            piece = ready(2 + at)[...]
        else:
            piece = jnp.concatenate([ready(9)[...], ready(10)[...]], axis=0)
        place = order[at]
        parent = split(
            jnp.concatenate([cols[place, 0:128, :], cols[place, 128:256, :]], axis=1)
        )
        for half in range(2):
            totals[half] += product(split(piece[half * 256 : (half + 1) * 256]), parent)
    for half in range(2):
        for leaf in range(2):
            out[leaf, half * 256 : (half + 1) * 256, :] = -totals[half][
                :, leaf * 128 : (leaf + 1) * 128
            ]


def parent_kernel(order, *refs):
    sources, out, scratch, sems = refs[:11], refs[11], refs[12:23], refs[23]
    ready = fetched(sources, scratch, sems)
    cols, cross = ready(0), ready(1)
    total = jnp.zeros((256, 256), jnp.float32)
    for at in range(8):
        if at < 7:
            piece = ready(2 + at)[...]
        else:
            piece = jnp.concatenate([ready(9)[...], ready(10)[...]], axis=0)
        place = order[at]
        parent = jnp.concatenate([cols[place, 0:128, :], cols[place, 128:256, :]], axis=1)
        total += product(split(piece), split(parent))
    for leaf in range(2):
        for sub in range(2):
            added = cross[0, sub, leaf]
            for y in range(1, SIZE_Y):
                added += cross[y, sub, leaf]
            rows = slice(sub * 128, (sub + 1) * 128)
            out[leaf, rows, :] = -(total[rows, leaf * 128 : (leaf + 1) * 128] + added)


def leaf_kernel(core, weight, parent, root, panels, out, total, high, low):
    block, half = pl.program_id(0), pl.program_id(1)

    @pl.when(block == 0)
    def _():
        for leaf in range(2):
            rows = jnp.concatenate([parent[leaf], root[leaf]], axis=0)
            high[half, leaf], low[half, leaf] = split(jnp.transpose(rows))

    for leaf in range(2):
        right = split(jnp.concatenate([panels[0, leaf], panels[1, leaf]], axis=1))
        part = product((high[half, leaf], low[half, leaf]), right)

        @pl.when(half == 0)
        def _():
            total[leaf] = part

        @pl.when(half == 1)
        def _():
            done = weight[0] * (total[leaf] + part)
            for side in range(2):
                out[:, 0, side, leaf] = done[:, side * 128 : (side + 1) * 128].reshape(
                    SIZE_X, 32, 128
                )


def leaf_cross(core, weight, parent, root, panels):
    return pl.pallas_call(
        leaf_kernel,
        out_shape=jax.ShapeDtypeStruct((SIZE_X, SIZE_Y, 2, 2, 32, 128), jnp.float32),
        grid_spec=pltpu.PrefetchScalarGridSpec(
            num_scalar_prefetch=1,
            grid=(SIZE_L, SIZE_H),
            in_specs=[
                IN_SMEM,
                pl.BlockSpec((2, 128, 128), lambda l, h, core: (0, h, 0)),
                pl.BlockSpec((2, 256, 128), lambda l, h, core: (0, h, 0)),
                pl.BlockSpec((2, 2, 384, 128), lambda l, h, core: (h * 4 + l, core[0], 0, 0)),
            ],
            out_specs=pl.BlockSpec(
                (SIZE_X, 1, 2, 2, 32, 128), lambda l, h, core: (0, l, 0, 0, 0, 0)
            ),
            scratch_shapes=[
                pltpu.VMEM((2, 128, 256), jnp.float32),
                pltpu.VMEM((2, 2, 128, 384), jnp.bfloat16),
                pltpu.VMEM((2, 2, 128, 384), jnp.bfloat16),
            ],
        ),
        cost_estimate=cost(2 * 768 * 1024 * 128, [(2, 768, 1024), (2, 768, 128), (2, 1024, 128)]),
        compiler_params=VMEM,
    )(core, weight, parent, root, panels)


def cost(terms, arrays):
    moved = 4 * sum(math.prod(shape) for shape in arrays)
    return pl.CostEstimate(flops=6 * terms, bytes_accessed=moved, transcendentals=0)


def with_copies(kernel, shapes, order, *operands, terms, copies=None):
    specs = [pl.BlockSpec(memory_space=pl.ANY)] * len(operands)
    scratch = [pltpu.VMEM(operand.shape, jnp.float32) for operand in operands]
    scratch.append(pltpu.SemaphoreType.DMA((copies or len(operands),)))
    price = cost(terms, [operand.shape for operand in operands] + shapes)
    if order is not None:
        specs, operands = [IN_SMEM] + specs, (order,) + operands
    return pl.pallas_call(
        kernel,
        out_shape=[jax.ShapeDtypeStruct(shape, jnp.float32) for shape in shapes],
        in_specs=specs,
        out_specs=[IN_VMEM] * len(shapes),
        scratch_shapes=scratch,
        cost_estimate=price,
        compiler_params=VMEM,
    )(*operands)


def body(
    root_inverse,
    top_factor,
    parent_factor,
    root_factor,
    top_pivots_inv,
    leaf_pivots_inv,
    pattern_top,
    pattern_parent,
    pattern_root,
    pole_weights,
):
    zh = lax.axis_index("zh")
    zl = lax.axis_index("zl")
    core = lax.axis_index("core")
    place = zh * SIZE_L + zl
    weight = pole_weights[0]

    top = top_factor[0] * block_mask(pattern_top, 256)[:, :, None]
    parent = parent_factor[0] * block_mask(pattern_parent, 128)[:, :, None]
    root = root_factor[0] * block_mask(pattern_root, 256)[:, :, None]

    leaves = jnp.concatenate([parent, root], axis=1)

    def to_ring(value):
        got = []
        for flip in range(2):
            piece = lax.dynamic_index_in_dim(value, zh ^ flip, 0, keepdims=False)
            got.append(
                lax.ppermute(piece, LANE, lane_pairs(lambda h, l, c: (c, l, h ^ flip)))
            )
        return jnp.stack(in_order(core, got[0], got[1]))

    inverse = lax.all_gather(root_inverse[0], LANE, axis=0)

    top_block = to_ring(jnp.concatenate([top, top_pivots_inv[0]], axis=1))
    top_block, parent, root = lax.optimization_barrier((top_block, parent, root))
    leaf_block = to_ring(
        jnp.concatenate([parent.reshape(2, 256, 128), root.reshape(2, 512, 128)], axis=1)
    )
    pivot_block = top_block[:, 256:].reshape(256, 128)
    top_block = top_block[:, :256]
    top_cols = spread(top_block, "y", SIZE_Y).reshape(8, 256, 128)
    leaf = (weight * leaf_pivots_inv[0]).reshape(4, SIZE_X, 32, 128)
    leaf = jnp.sum(lax.all_to_all(jnp.moveaxis(leaf, 1, 0), "pole", 0, 0), axis=0)
    top_cols, leaf, leaf_block = lax.optimization_barrier((top_cols, leaf, leaf_block))
    inverse, leaf_block = lax.optimization_barrier((inverse, leaf_block))
    leaf_cols = lax.all_gather(leaf_block, "y", axis=0).reshape(8, 768, 128)

    (outer,) = with_copies(
        outer_kernel,
        [(512, 128)],
        None,
        inverse,
        top_cols,
        terms=512 * 2048 * 128,
        copies=17,
    )
    pieces = [outer]
    for step in range(3):
        pieces += onward(pieces, step)
    pieces[5], pieces[6], leaves, leaf_cols = lax.optimization_barrier(
        (pieces[5], pieces[6], leaves, leaf_cols)
    )
    panels = lax.all_gather(leaves, LANE, axis=0)
    pieces += onward(pieces, 3)
    order = jnp.stack([column_of((place + d) % SIZE_Z) for d in (0, 7, 1, 6, 2, 5, 3, 4)])

    cross_top, cross_leaf = with_copies(
        cross_kernel,
        [(8, 128, 128), (8, 2, 128, 128)],
        order,
        top_block,
        leaf_block,
        *pieces,
        terms=512 * 1024 * 384,
    )
    cross_leaf, leaf_cols = lax.optimization_barrier((cross_leaf, leaf_cols))
    (leaf_root,) = with_copies(
        root_kernel,
        [(2, 512, 128)],
        order,
        leaf_cols,
        inverse,
        *pieces,
        terms=512 * 3072 * 256,
    )
    cross_top = lax.all_to_all(cross_top.reshape(SIZE_Y, 256, 128), "y", 0, 0)
    cross_top, cross_leaf, leaf_root = lax.optimization_barrier(
        (cross_top, cross_leaf, leaf_root)
    )
    cross_leaf = lax.all_to_all(cross_leaf.reshape(SIZE_Y, 2, 2, 128, 128), "y", 0, 0)
    top_diag = pivot_block - jnp.sum(cross_top, axis=0)
    def summed(values):
        blocks = jnp.concatenate(
            [value.reshape(SIZE_H, value.shape[0] // SIZE_H, 128) for value in values], axis=1
        )
        blocks = (weight * blocks).reshape(SIZE_H, SIZE_X, blocks.shape[1] // SIZE_X, 128)
        return jnp.sum(lax.all_to_all(jnp.moveaxis(blocks, 1, 0), "pole", 0, 0), axis=0)

    def in_place(blocks):
        got = []
        for flip in range(2):
            piece = lax.dynamic_index_in_dim(blocks, core ^ flip, 0, keepdims=False)
            got.append(
                lax.ppermute(piece, LANE, lane_pairs(lambda h, l, c: (c ^ flip, l, h)))
            )
        return jnp.stack(in_order(zh, got[0], got[1]), axis=0)

    def everywhere(pair):
        every = jnp.moveaxis(spread(pair, "pole", SIZE_X), 0, 1)
        return every.reshape(pair.shape[0], SIZE_X * pair.shape[1], 128)

    diag_pieces = [top_diag]
    for step in range(3):
        diag_pieces += onward(diag_pieces, step)
    early = summed([outer, leaf_root[0], leaf_root[1]])
    diag_pieces[5], diag_pieces[6], early = lax.optimization_barrier(
        (diag_pieces[5], diag_pieces[6], early)
    )
    diag_pieces += onward(diag_pieces, 3)
    early = in_place(early)
    diag_pieces[7], diag_pieces[8], early = lax.optimization_barrier(
        (diag_pieces[7], diag_pieces[8], early)
    )
    (leaf_parent,) = with_copies(
        parent_kernel,
        [(2, 256, 128)],
        order,
        leaf_cols,
        cross_leaf,
        *diag_pieces,
        terms=256 * 1024 * 256,
    )
    early = everywhere(early)
    late = summed([top_diag, leaf_parent[0], leaf_parent[1]])

    cross = leaf_cross(core.reshape(1), pole_weights, leaf_parent, leaf_root, panels)
    cross, early = lax.optimization_barrier((cross, early))
    cross = cross.reshape(SIZE_X * SIZE_Y, 2, 2, 32, 128)
    cross = jnp.sum(lax.all_to_all(cross, ("pole", "y"), 0, 0), axis=0)
    late = in_place(late)
    got = []
    for flip in range(2):
        piece = lax.dynamic_index_in_dim(cross, core ^ flip, 0, keepdims=False)
        got.append(lax.ppermute(piece, PLANE, plane_pairs(flip)))
    cross = jnp.concatenate(in_order(core, got[0], got[1]), axis=0)
    ends = everywhere(jnp.concatenate([late.reshape(6, 32, 128), leaf - cross], axis=0))
    outer_dens = early[:, :256]
    rootward_dens = early[:, 256:].reshape(4, 256, 128)
    leaf_dens = ends[6:]
    late = jnp.moveaxis(ends[:6].reshape(2, 3, SIZE_X, 32, 128), 2, 1).reshape(2, 384, 128)
    top_dens = late[:, :128]
    parent_dens = late[:, 128:].reshape(4, 128, 128)
    return (top_dens, outer_dens, leaf_dens, parent_dens, rootward_dens)


def solution(mesh):
    fine = Mesh(
        mesh.devices.reshape(SIZE_X, SIZE_Y, SIZE_H, SIZE_L, SIZE_C),
        ("pole", "y", "zh", "zl", "core"),
    )
    row, col = ("y", "zh"), ("zl", "core")
    return jax.shard_map(
        body,
        mesh=fine,
        in_specs=(
            P("pole", row, col),
            P("pole", None, row, col),
            P("pole", None, row, col),
            P("pole", None, row, col),
            P("pole", None, row, col),
            P("pole", None, row, col),
            P(None, row),
            P(None, row),
            P(None, row),
            P("pole"),
        ),
        out_specs=(
            P(None, row, col),
            P(None, row, col),
            P(None, row, col),
            P(None, row, col),
            P(None, row, col),
        ),
        check_vma=False,
    )
```

```python
import math

import jax
import jax.numpy as jnp
from jax import lax
from jax.experimental import pallas as pl
from jax.experimental.pallas import tpu as pltpu
from jax.sharding import Mesh
from jax.sharding import PartitionSpec as P

RING = ("zh", "zl")
LANE = ("zh", "zl", "core")
PLANE = ("y", "zh", "zl", "core")
SIZE_X, SIZE_Y, SIZE_H, SIZE_L, SIZE_C = 4, 4, 2, 4, 2
SIZE_Z = SIZE_H * SIZE_L
VMEM = pltpu.CompilerParams(vmem_limit_bytes=64 * 1024 * 1024)
IN_VMEM = pl.BlockSpec(memory_space=pltpu.VMEM)
IN_SMEM = pl.BlockSpec(memory_space=pltpu.SMEM)


def block_mask(pattern, rows):
    width = rows // pattern.shape[-1]
    return jnp.repeat(pattern.astype(jnp.float32), width, axis=-1)


def lane_pairs(target):
    pairs = []
    for zh in range(SIZE_H):
        for zl in range(SIZE_L):
            for core in range(SIZE_C):
                to_h, to_l, to_c = target(zh, zl, core)
                pairs.append(
                    ((zh * SIZE_L + zl) * SIZE_C + core, (to_h * SIZE_L + to_l) * SIZE_C + to_c)
                )
    return pairs


def plane_pairs(flip):
    pairs = []
    for y in range(SIZE_Y):
        for zh in range(SIZE_H):
            for zl in range(SIZE_L):
                for core in range(SIZE_C):
                    here = ((y * SIZE_H + zh) * SIZE_L + zl) * SIZE_C + core
                    there = ((zl * SIZE_H + zh) * SIZE_L + y) * SIZE_C + (core ^ flip)
                    pairs.append((here, there))
    return pairs


def ring_pairs(step):
    return [(z, (z + step) % SIZE_Z) for z in range(SIZE_Z)]


def onward(pieces, step):
    ahead, behind = (pieces[-2], pieces[-1]) if step else (pieces[0], pieces[0])
    if step == 3:
        half = ahead.shape[0] // 2
        ahead, behind = ahead[:half], behind[half:]
    return [
        lax.ppermute(ahead, RING, ring_pairs(1)),
        lax.ppermute(behind, RING, ring_pairs(-1)),
    ]


def column_of(place):
    return (place % SIZE_L) * SIZE_H + place // SIZE_L


def spread(value, axis, size):
    return lax.all_to_all(jnp.broadcast_to(value[None], (size,) + value.shape), axis, 0, 0)


def in_order(flag, first, second):
    return jnp.where(flag == 0, first, second), jnp.where(flag == 0, second, first)


def split(value):
    high = value.astype(jnp.bfloat16)
    return high, (value - high.astype(jnp.float32)).astype(jnp.bfloat16)


def product(left, right, dims=((1,), (0,))):
    def one(a, b):
        return lax.dot_general(a, b, (dims, ((), ())), preferred_element_type=jnp.float32)

    return one(left[0], right[0]) + (one(left[0], right[1]) + one(left[1], right[0]))


def product_t(left, right):
    return product(left, right, ((0,), (0,)))


def fetched(sources, scratch, sems):
    copies = [
        pltpu.make_async_copy(source, to, sems.at[at])
        for at, (source, to) in enumerate(zip(sources, scratch))
    ]
    for copy in copies:
        copy.start()

    def ready(at):
        copies[at].wait()
        return scratch[at]

    return ready


def outer_kernel(inverse, top, out, inverse_here, top_here, sems):
    order = [half * 8 + k for k in range(8) for half in range(2)]
    ready = fetched(
        [top] + [inverse.at[at] for at in order],
        [top_here] + [inverse_here.at[at] for at in order],
        sems,
    )
    ready(0)
    totals = [None, None]
    for k in range(8):
        right = split(top_here[k])
        for half in range(2):
            left = split(ready(1 + k * 2 + half)[...])
            part = product(left, right)
            totals[half] = part if k == 0 else totals[half] + part
    for half in range(2):
        out[half * 256 : (half + 1) * 256, :] = -totals[half]


def cross_kernel(order, *refs):
    sources, (top_out, leaf_out) = refs[:11], refs[11:13]
    scratch, sems = refs[13:24], refs[24]
    ready = fetched(sources, scratch, sems)
    top, mine = ready(0), ready(1)
    panels = split(
        jnp.concatenate(
            [
                jnp.concatenate([top[zh], mine[zh, 256:512, :], mine[zh, 512:768, :]], axis=1)
                for zh in range(SIZE_H)
            ],
            axis=0,
        )
    )
    for at in range(8):
        if at < 7:
            piece = ready(2 + at)[...]
        else:
            piece = jnp.concatenate([ready(9)[...], ready(10)[...]], axis=0)
        part = product_t(split(piece), panels)
        top_out[order[at]] = part[:, :128]
        leaf_out[order[at], 0] = part[:, 128:256]
        leaf_out[order[at], 1] = part[:, 256:]


def root_kernel(order, *refs):
    sources, out = refs[:11], refs[11]
    scratch, sems = refs[12:23], refs[23]
    ready = fetched(sources, scratch, sems)
    cols, inverse = ready(0), ready(1)
    totals = [jnp.zeros((256, 256), jnp.float32) for _ in range(2)]
    for k in range(8):
        root = split(jnp.concatenate([cols[k, 256:512, :], cols[k, 512:768, :]], axis=1))
        for half in range(2):
            totals[half] += product(split(inverse[half * 8 + k]), root)
    for at in range(8):
        if at < 7:
            piece = ready(2 + at)[...]
        else:
            piece = jnp.concatenate([ready(9)[...], ready(10)[...]], axis=0)
        place = order[at]
        parent = split(
            jnp.concatenate([cols[place, 0:128, :], cols[place, 128:256, :]], axis=1)
        )
        for half in range(2):
            totals[half] += product(split(piece[half * 256 : (half + 1) * 256]), parent)
    for half in range(2):
        for leaf in range(2):
            out[leaf, half * 256 : (half + 1) * 256, :] = -totals[half][
                :, leaf * 128 : (leaf + 1) * 128
            ]


def parent_kernel(order, *refs):
    sources, out, scratch, sems = refs[:11], refs[11], refs[12:23], refs[23]
    ready = fetched(sources, scratch, sems)
    cols, cross = ready(0), ready(1)
    total = jnp.zeros((256, 256), jnp.float32)
    for at in range(8):
        if at < 7:
            piece = ready(2 + at)[...]
        else:
            piece = jnp.concatenate([ready(9)[...], ready(10)[...]], axis=0)
        place = order[at]
        parent = jnp.concatenate([cols[place, 0:128, :], cols[place, 128:256, :]], axis=1)
        total += product(split(piece), split(parent))
    for leaf in range(2):
        for sub in range(2):
            added = cross[0, sub, leaf]
            for y in range(1, SIZE_Y):
                added += cross[y, sub, leaf]
            rows = slice(sub * 128, (sub + 1) * 128)
            out[leaf, rows, :] = -(total[rows, leaf * 128 : (leaf + 1) * 128] + added)


def leaf_kernel(core, weight, parent, root, panels, out, total, high, low):
    block, half = pl.program_id(0), pl.program_id(1)

    @pl.when(block == 0)
    def _():
        for leaf in range(2):
            rows = jnp.concatenate([parent[leaf], root[leaf]], axis=0)
            high[half, leaf], low[half, leaf] = split(jnp.transpose(rows))

    for leaf in range(2):
        right = split(jnp.concatenate([panels[0, leaf], panels[1, leaf]], axis=1))
        part = product((high[half, leaf], low[half, leaf]), right)

        @pl.when(half == 0)
        def _():
            total[leaf] = part

        @pl.when(half == 1)
        def _():
            done = weight[0] * (total[leaf] + part)
            for side in range(2):
                out[:, 0, side, leaf] = done[:, side * 128 : (side + 1) * 128].reshape(
                    SIZE_X, 32, 128
                )


def leaf_cross(core, weight, parent, root, panels):
    return pl.pallas_call(
        leaf_kernel,
        out_shape=jax.ShapeDtypeStruct((SIZE_X, SIZE_Y, 2, 2, 32, 128), jnp.float32),
        grid_spec=pltpu.PrefetchScalarGridSpec(
            num_scalar_prefetch=1,
            grid=(SIZE_L, SIZE_H),
            in_specs=[
                IN_SMEM,
                pl.BlockSpec((2, 128, 128), lambda l, h, core: (0, h, 0)),
                pl.BlockSpec((2, 256, 128), lambda l, h, core: (0, h, 0)),
                pl.BlockSpec((2, 2, 384, 128), lambda l, h, core: (h * 4 + l, core[0], 0, 0)),
            ],
            out_specs=pl.BlockSpec(
                (SIZE_X, 1, 2, 2, 32, 128), lambda l, h, core: (0, l, 0, 0, 0, 0)
            ),
            scratch_shapes=[
                pltpu.VMEM((2, 128, 256), jnp.float32),
                pltpu.VMEM((2, 2, 128, 384), jnp.bfloat16),
                pltpu.VMEM((2, 2, 128, 384), jnp.bfloat16),
            ],
        ),
        cost_estimate=cost(2 * 768 * 1024 * 128, [(2, 768, 1024), (2, 768, 128), (2, 1024, 128)]),
        compiler_params=VMEM,
    )(core, weight, parent, root, panels)


def cost(terms, arrays):
    moved = 4 * sum(math.prod(shape) for shape in arrays)
    return pl.CostEstimate(flops=6 * terms, bytes_accessed=moved, transcendentals=0)


def with_copies(kernel, shapes, order, *operands, terms, copies=None):
    specs = [pl.BlockSpec(memory_space=pl.ANY)] * len(operands)
    scratch = [pltpu.VMEM(operand.shape, jnp.float32) for operand in operands]
    scratch.append(pltpu.SemaphoreType.DMA((copies or len(operands),)))
    price = cost(terms, [operand.shape for operand in operands] + shapes)
    if order is not None:
        specs, operands = [IN_SMEM] + specs, (order,) + operands
    return pl.pallas_call(
        kernel,
        out_shape=[jax.ShapeDtypeStruct(shape, jnp.float32) for shape in shapes],
        in_specs=specs,
        out_specs=[IN_VMEM] * len(shapes),
        scratch_shapes=scratch,
        cost_estimate=price,
        compiler_params=VMEM,
    )(*operands)


def body(
    root_inverse,
    top_factor,
    parent_factor,
    root_factor,
    top_pivots_inv,
    leaf_pivots_inv,
    pattern_top,
    pattern_parent,
    pattern_root,
    pole_weights,
):
    zh = lax.axis_index("zh")
    zl = lax.axis_index("zl")
    core = lax.axis_index("core")
    place = zh * SIZE_L + zl
    weight = pole_weights[0]

    top = top_factor[0] * block_mask(pattern_top, 256)[:, :, None]
    parent = parent_factor[0] * block_mask(pattern_parent, 128)[:, :, None]
    root = root_factor[0] * block_mask(pattern_root, 256)[:, :, None]

    leaves = jnp.concatenate([parent, root], axis=1)

    def to_ring(value):
        got = []
        for flip in range(2):
            piece = lax.dynamic_index_in_dim(value, zh ^ flip, 0, keepdims=False)
            got.append(
                lax.ppermute(piece, LANE, lane_pairs(lambda h, l, c: (c, l, h ^ flip)))
            )
        return jnp.stack(in_order(core, got[0], got[1]))

    inverse = lax.all_gather(root_inverse[0], LANE, axis=0)

    top_block = to_ring(jnp.concatenate([top, top_pivots_inv[0]], axis=1))
    top_block, parent, root = lax.optimization_barrier((top_block, parent, root))
    leaf_block = to_ring(
        jnp.concatenate([parent.reshape(2, 256, 128), root.reshape(2, 512, 128)], axis=1)
    )
    pivot_block = top_block[:, 256:].reshape(256, 128)
    top_block = top_block[:, :256]
    top_cols = spread(top_block, "y", SIZE_Y).reshape(8, 256, 128)
    leaf = (weight * leaf_pivots_inv[0]).reshape(4, SIZE_X, 32, 128)
    leaf = jnp.sum(lax.all_to_all(jnp.moveaxis(leaf, 1, 0), "pole", 0, 0), axis=0)
    top_cols, leaf, leaf_block = lax.optimization_barrier((top_cols, leaf, leaf_block))
    inverse, leaf_block = lax.optimization_barrier((inverse, leaf_block))
    leaf_cols = lax.all_gather(leaf_block, "y", axis=0).reshape(8, 768, 128)

    (outer,) = with_copies(
        outer_kernel,
        [(512, 128)],
        None,
        inverse,
        top_cols,
        terms=512 * 2048 * 128,
        copies=17,
    )
    pieces = [outer]
    for step in range(3):
        pieces += onward(pieces, step)
    pieces += onward(pieces, 3)
    pieces[7], pieces[8], leaves = lax.optimization_barrier((pieces[7], pieces[8], leaves))
    panels = lax.all_gather(leaves, LANE, axis=0)
    order = jnp.stack([column_of((place + d) % SIZE_Z) for d in (0, 7, 1, 6, 2, 5, 3, 4)])

    cross_top, cross_leaf = with_copies(
        cross_kernel,
        [(8, 128, 128), (8, 2, 128, 128)],
        order,
        top_block,
        leaf_block,
        *pieces,
        terms=512 * 1024 * 384,
    )
    cross_leaf, leaf_cols = lax.optimization_barrier((cross_leaf, leaf_cols))
    (leaf_root,) = with_copies(
        root_kernel,
        [(2, 512, 128)],
        order,
        leaf_cols,
        inverse,
        *pieces,
        terms=512 * 3072 * 256,
    )
    cross_top = lax.all_to_all(cross_top.reshape(SIZE_Y, 256, 128), "y", 0, 0)
    cross_top, cross_leaf, leaf_root = lax.optimization_barrier(
        (cross_top, cross_leaf, leaf_root)
    )
    cross_leaf = lax.all_to_all(cross_leaf.reshape(SIZE_Y, 2, 2, 128, 128), "y", 0, 0)
    top_diag = pivot_block - jnp.sum(cross_top, axis=0)
    def summed(values):
        blocks = jnp.concatenate(
            [value.reshape(SIZE_H, value.shape[0] // SIZE_H, 128) for value in values], axis=1
        )
        blocks = (weight * blocks).reshape(SIZE_H, SIZE_X, blocks.shape[1] // SIZE_X, 128)
        return jnp.sum(lax.all_to_all(jnp.moveaxis(blocks, 1, 0), "pole", 0, 0), axis=0)

    def in_place(blocks):
        got = []
        for flip in range(2):
            piece = lax.dynamic_index_in_dim(blocks, core ^ flip, 0, keepdims=False)
            got.append(
                lax.ppermute(piece, LANE, lane_pairs(lambda h, l, c: (c ^ flip, l, h)))
            )
        return jnp.stack(in_order(zh, got[0], got[1]), axis=0)

    def everywhere(pair):
        every = jnp.moveaxis(spread(pair, "pole", SIZE_X), 0, 1)
        return every.reshape(pair.shape[0], SIZE_X * pair.shape[1], 128)

    diag_pieces = [top_diag]
    for step in range(3):
        diag_pieces += onward(diag_pieces, step)
    early = summed([outer, leaf_root[0], leaf_root[1], top_diag])
    diag_pieces[5], diag_pieces[6], early = lax.optimization_barrier(
        (diag_pieces[5], diag_pieces[6], early)
    )
    diag_pieces += onward(diag_pieces, 3)
    early = in_place(early)
    diag_pieces[7], diag_pieces[8], early = lax.optimization_barrier(
        (diag_pieces[7], diag_pieces[8], early)
    )
    (leaf_parent,) = with_copies(
        parent_kernel,
        [(2, 256, 128)],
        order,
        leaf_cols,
        cross_leaf,
        *diag_pieces,
        terms=256 * 1024 * 256,
    )
    early = everywhere(early)
    late = summed([leaf_parent[0], leaf_parent[1]])

    cross = leaf_cross(core.reshape(1), pole_weights, leaf_parent, leaf_root, panels)
    cross, early = lax.optimization_barrier((cross, early))
    cross = cross.reshape(SIZE_X * SIZE_Y, 2, 2, 32, 128)
    cross = jnp.sum(lax.all_to_all(cross, ("pole", "y"), 0, 0), axis=0)
    late = in_place(late)
    got = []
    for flip in range(2):
        piece = lax.dynamic_index_in_dim(cross, core ^ flip, 0, keepdims=False)
        got.append(lax.ppermute(piece, PLANE, plane_pairs(flip)))
    cross = jnp.concatenate(in_order(core, got[0], got[1]), axis=0)
    ends = everywhere(jnp.concatenate([late.reshape(4, 32, 128), leaf - cross], axis=0))
    outer_dens = early[:, :256]
    rootward_dens = early[:, 256:768].reshape(4, 256, 128)
    top_dens = early[:, 768:]
    leaf_dens = ends[4:]
    parent_dens = jnp.moveaxis(ends[:4].reshape(2, 2, SIZE_X, 32, 128), 2, 1)
    parent_dens = parent_dens.reshape(4, 128, 128)
    return (top_dens, outer_dens, leaf_dens, parent_dens, rootward_dens)


def solution(mesh):
    fine = Mesh(
        mesh.devices.reshape(SIZE_X, SIZE_Y, SIZE_H, SIZE_L, SIZE_C),
        ("pole", "y", "zh", "zl", "core"),
    )
    row, col = ("y", "zh"), ("zl", "core")
    return jax.shard_map(
        body,
        mesh=fine,
        in_specs=(
            P("pole", row, col),
            P("pole", None, row, col),
            P("pole", None, row, col),
            P("pole", None, row, col),
            P("pole", None, row, col),
            P("pole", None, row, col),
            P(None, row),
            P(None, row),
            P(None, row),
            P("pole"),
        ),
        out_specs=(
            P(None, row, col),
            P(None, row, col),
            P(None, row, col),
            P(None, row, col),
            P(None, row, col),
        ),
        check_vma=False,
    )
```

```python
import math

import jax
import jax.numpy as jnp
from jax import lax
from jax.experimental import pallas as pl
from jax.experimental.pallas import tpu as pltpu
from jax.sharding import Mesh
from jax.sharding import PartitionSpec as P

RING = ("zh", "zl")
LANE = ("zh", "zl", "core")
PLANE = ("y", "zh", "zl", "core")
SIZE_X, SIZE_Y, SIZE_H, SIZE_L, SIZE_C = 4, 4, 2, 4, 2
SIZE_Z = SIZE_H * SIZE_L
VMEM = pltpu.CompilerParams(vmem_limit_bytes=64 * 1024 * 1024)
IN_VMEM = pl.BlockSpec(memory_space=pltpu.VMEM)
IN_SMEM = pl.BlockSpec(memory_space=pltpu.SMEM)


def block_mask(pattern, rows):
    width = rows // pattern.shape[-1]
    return jnp.repeat(pattern.astype(jnp.float32), width, axis=-1)


def lane_pairs(target):
    pairs = []
    for zh in range(SIZE_H):
        for zl in range(SIZE_L):
            for core in range(SIZE_C):
                to_h, to_l, to_c = target(zh, zl, core)
                pairs.append(
                    ((zh * SIZE_L + zl) * SIZE_C + core, (to_h * SIZE_L + to_l) * SIZE_C + to_c)
                )
    return pairs


def plane_pairs(flip):
    pairs = []
    for y in range(SIZE_Y):
        for zh in range(SIZE_H):
            for zl in range(SIZE_L):
                for core in range(SIZE_C):
                    here = ((y * SIZE_H + zh) * SIZE_L + zl) * SIZE_C + core
                    there = ((zl * SIZE_H + zh) * SIZE_L + y) * SIZE_C + (core ^ flip)
                    pairs.append((here, there))
    return pairs


def ring_pairs(step):
    return [(z, (z + step) % SIZE_Z) for z in range(SIZE_Z)]


def onward(pieces, step):
    ahead, behind = (pieces[-2], pieces[-1]) if step else (pieces[0], pieces[0])
    if step == 3:
        half = ahead.shape[0] // 2
        ahead, behind = ahead[:half], behind[half:]
    return [
        lax.ppermute(ahead, RING, ring_pairs(1)),
        lax.ppermute(behind, RING, ring_pairs(-1)),
    ]


def column_of(place):
    return (place % SIZE_L) * SIZE_H + place // SIZE_L


def spread(value, axis, size):
    return lax.all_to_all(jnp.broadcast_to(value[None], (size,) + value.shape), axis, 0, 0)


def in_order(flag, first, second):
    return jnp.where(flag == 0, first, second), jnp.where(flag == 0, second, first)


def split(value):
    high = value.astype(jnp.bfloat16)
    return high, (value - high.astype(jnp.float32)).astype(jnp.bfloat16)


def product(left, right, dims=((1,), (0,))):
    def one(a, b):
        return lax.dot_general(a, b, (dims, ((), ())), preferred_element_type=jnp.float32)

    return one(left[0], right[0]) + (one(left[0], right[1]) + one(left[1], right[0]))


def product_t(left, right):
    return product(left, right, ((0,), (0,)))


def fetched(sources, scratch, sems):
    copies = [
        pltpu.make_async_copy(source, to, sems.at[at])
        for at, (source, to) in enumerate(zip(sources, scratch))
    ]
    for copy in copies:
        copy.start()

    def ready(at):
        copies[at].wait()
        return scratch[at]

    return ready


def outer_kernel(inverse, top, out, inverse_here, top_here, sems):
    order = [half * 8 + k for k in range(8) for half in range(2)]
    ready = fetched(
        [top] + [inverse.at[at] for at in order],
        [top_here] + [inverse_here.at[at] for at in order],
        sems,
    )
    ready(0)
    totals = [None, None]
    for k in range(8):
        right = split(top_here[k])
        for half in range(2):
            left = split(ready(1 + k * 2 + half)[...])
            part = product(left, right)
            totals[half] = part if k == 0 else totals[half] + part
    for half in range(2):
        out[half * 256 : (half + 1) * 256, :] = -totals[half]


def cross_kernel(order, *refs):
    sources, (top_out, leaf_out) = refs[:11], refs[11:13]
    scratch, sems = refs[13:24], refs[24]
    ready = fetched(sources, scratch, sems)
    top, mine = ready(0), ready(1)
    panels = split(
        jnp.concatenate(
            [
                jnp.concatenate([top[zh], mine[zh, 256:512, :], mine[zh, 512:768, :]], axis=1)
                for zh in range(SIZE_H)
            ],
            axis=0,
        )
    )
    for at in range(8):
        if at < 7:
            piece = ready(2 + at)[...]
        else:
            piece = jnp.concatenate([ready(9)[...], ready(10)[...]], axis=0)
        part = product_t(split(piece), panels)
        top_out[order[at]] = part[:, :128]
        leaf_out[order[at], 0] = part[:, 128:256]
        leaf_out[order[at], 1] = part[:, 256:]


def root_kernel(order, *refs):
    sources, out = refs[:11], refs[11]
    scratch, sems = refs[12:23], refs[23]
    ready = fetched(sources, scratch, sems)
    cols, inverse = ready(0), ready(1)
    totals = [jnp.zeros((256, 256), jnp.float32) for _ in range(2)]
    for k in range(8):
        root = split(jnp.concatenate([cols[k, 256:512, :], cols[k, 512:768, :]], axis=1))
        for half in range(2):
            totals[half] += product(split(inverse[half * 8 + k]), root)
    for at in range(8):
        if at < 7:
            piece = ready(2 + at)[...]
        else:
            piece = jnp.concatenate([ready(9)[...], ready(10)[...]], axis=0)
        place = order[at]
        parent = split(
            jnp.concatenate([cols[place, 0:128, :], cols[place, 128:256, :]], axis=1)
        )
        for half in range(2):
            totals[half] += product(split(piece[half * 256 : (half + 1) * 256]), parent)
    for half in range(2):
        for leaf in range(2):
            out[leaf, half * 256 : (half + 1) * 256, :] = -totals[half][
                :, leaf * 128 : (leaf + 1) * 128
            ]


def parent_kernel(order, *refs):
    sources, out, scratch, sems = refs[:11], refs[11], refs[12:23], refs[23]
    ready = fetched(sources, scratch, sems)
    cols, cross = ready(0), ready(1)
    total = jnp.zeros((256, 256), jnp.float32)
    for at in range(8):
        if at < 7:
            piece = ready(2 + at)[...]
        else:
            piece = jnp.concatenate([ready(9)[...], ready(10)[...]], axis=0)
        place = order[at]
        parent = jnp.concatenate([cols[place, 0:128, :], cols[place, 128:256, :]], axis=1)
        total += product(split(piece), split(parent))
    for leaf in range(2):
        for sub in range(2):
            added = cross[0, sub, leaf]
            for y in range(1, SIZE_Y):
                added += cross[y, sub, leaf]
            rows = slice(sub * 128, (sub + 1) * 128)
            out[leaf, rows, :] = -(total[rows, leaf * 128 : (leaf + 1) * 128] + added)


def leaf_kernel(core, weight, parent, root, panels, out, total, high, low):
    block, half = pl.program_id(0), pl.program_id(1)

    @pl.when(block == 0)
    def _():
        for leaf in range(2):
            rows = jnp.concatenate([parent[leaf], root[leaf]], axis=0)
            high[half, leaf], low[half, leaf] = split(jnp.transpose(rows))

    for leaf in range(2):
        right = split(jnp.concatenate([panels[0, leaf], panels[1, leaf]], axis=1))
        part = product((high[half, leaf], low[half, leaf]), right)

        @pl.when(half == 0)
        def _():
            total[leaf] = part

        @pl.when(half == 1)
        def _():
            done = weight[0] * (total[leaf] + part)
            for side in range(2):
                out[:, 0, side, leaf] = done[:, side * 128 : (side + 1) * 128].reshape(
                    SIZE_X, 32, 128
                )


def leaf_cross(core, weight, parent, root, panels):
    return pl.pallas_call(
        leaf_kernel,
        out_shape=jax.ShapeDtypeStruct((SIZE_X, SIZE_Y, 2, 2, 32, 128), jnp.float32),
        grid_spec=pltpu.PrefetchScalarGridSpec(
            num_scalar_prefetch=1,
            grid=(SIZE_L, SIZE_H),
            in_specs=[
                IN_SMEM,
                pl.BlockSpec((2, 128, 128), lambda l, h, core: (0, h, 0)),
                pl.BlockSpec((2, 256, 128), lambda l, h, core: (0, h, 0)),
                pl.BlockSpec((2, 2, 384, 128), lambda l, h, core: (h * 4 + l, core[0], 0, 0)),
            ],
            out_specs=pl.BlockSpec(
                (SIZE_X, 1, 2, 2, 32, 128), lambda l, h, core: (0, l, 0, 0, 0, 0)
            ),
            scratch_shapes=[
                pltpu.VMEM((2, 128, 256), jnp.float32),
                pltpu.VMEM((2, 2, 128, 384), jnp.bfloat16),
                pltpu.VMEM((2, 2, 128, 384), jnp.bfloat16),
            ],
        ),
        cost_estimate=cost(2 * 768 * 1024 * 128, [(2, 768, 1024), (2, 768, 128), (2, 1024, 128)]),
        compiler_params=VMEM,
    )(core, weight, parent, root, panels)


def cost(terms, arrays):
    moved = 4 * sum(math.prod(shape) for shape in arrays)
    return pl.CostEstimate(flops=6 * terms, bytes_accessed=moved, transcendentals=0)


def with_copies(kernel, shapes, order, *operands, terms, copies=None):
    specs = [pl.BlockSpec(memory_space=pl.ANY)] * len(operands)
    scratch = [pltpu.VMEM(operand.shape, jnp.float32) for operand in operands]
    scratch.append(pltpu.SemaphoreType.DMA((copies or len(operands),)))
    price = cost(terms, [operand.shape for operand in operands] + shapes)
    if order is not None:
        specs, operands = [IN_SMEM] + specs, (order,) + operands
    return pl.pallas_call(
        kernel,
        out_shape=[jax.ShapeDtypeStruct(shape, jnp.float32) for shape in shapes],
        in_specs=specs,
        out_specs=[IN_VMEM] * len(shapes),
        scratch_shapes=scratch,
        cost_estimate=price,
        compiler_params=VMEM,
    )(*operands)


def body(
    root_inverse,
    top_factor,
    parent_factor,
    root_factor,
    top_pivots_inv,
    leaf_pivots_inv,
    pattern_top,
    pattern_parent,
    pattern_root,
    pole_weights,
):
    zh = lax.axis_index("zh")
    zl = lax.axis_index("zl")
    core = lax.axis_index("core")
    place = zh * SIZE_L + zl
    weight = pole_weights[0]

    top = top_factor[0] * block_mask(pattern_top, 256)[:, :, None]
    parent = parent_factor[0] * block_mask(pattern_parent, 128)[:, :, None]
    root = root_factor[0] * block_mask(pattern_root, 256)[:, :, None]

    leaves = jnp.concatenate([parent, root], axis=1)

    def to_ring(value):
        got = []
        for flip in range(2):
            piece = lax.dynamic_index_in_dim(value, zh ^ flip, 0, keepdims=False)
            got.append(
                lax.ppermute(piece, LANE, lane_pairs(lambda h, l, c: (c, l, h ^ flip)))
            )
        return jnp.stack(in_order(core, got[0], got[1]))

    inverse = lax.all_gather(root_inverse[0], LANE, axis=0)

    top_block = to_ring(jnp.concatenate([top, top_pivots_inv[0]], axis=1))
    top_block, parent, root = lax.optimization_barrier((top_block, parent, root))
    leaf_block = to_ring(
        jnp.concatenate([parent.reshape(2, 256, 128), root.reshape(2, 512, 128)], axis=1)
    )
    pivot_block = top_block[:, 256:].reshape(256, 128)
    top_block = top_block[:, :256]
    top_cols = spread(top_block, "y", SIZE_Y).reshape(8, 256, 128)
    leaf = (weight * leaf_pivots_inv[0]).reshape(4, SIZE_X, 32, 128)
    leaf = jnp.sum(lax.all_to_all(jnp.moveaxis(leaf, 1, 0), "pole", 0, 0), axis=0)
    top_cols, leaf, leaf_block = lax.optimization_barrier((top_cols, leaf, leaf_block))
    inverse, leaf_block = lax.optimization_barrier((inverse, leaf_block))
    leaf_cols = lax.all_gather(leaf_block, "y", axis=0).reshape(8, 768, 128)

    (outer,) = with_copies(
        outer_kernel,
        [(512, 128)],
        None,
        inverse,
        top_cols,
        terms=512 * 2048 * 128,
        copies=17,
    )
    pieces = [outer]
    for step in range(3):
        pieces += onward(pieces, step)
    pieces += onward(pieces, 3)
    pieces[7], pieces[8], leaves = lax.optimization_barrier((pieces[7], pieces[8], leaves))
    panels = lax.all_gather(leaves, LANE, axis=0)
    order = jnp.stack([column_of((place + d) % SIZE_Z) for d in (0, 7, 1, 6, 2, 5, 3, 4)])

    cross_top, cross_leaf = with_copies(
        cross_kernel,
        [(8, 128, 128), (8, 2, 128, 128)],
        order,
        top_block,
        leaf_block,
        *pieces,
        terms=512 * 1024 * 384,
    )
    cross_leaf, leaf_cols = lax.optimization_barrier((cross_leaf, leaf_cols))
    (leaf_root,) = with_copies(
        root_kernel,
        [(2, 512, 128)],
        order,
        leaf_cols,
        inverse,
        *pieces,
        terms=512 * 3072 * 256,
    )
    cross_top = lax.all_to_all(cross_top.reshape(SIZE_Y, 256, 128), "y", 0, 0)
    cross_top, cross_leaf, leaf_root = lax.optimization_barrier(
        (cross_top, cross_leaf, leaf_root)
    )
    cross_leaf = lax.all_to_all(cross_leaf.reshape(SIZE_Y, 2, 2, 128, 128), "y", 0, 0)
    top_diag = pivot_block - jnp.sum(cross_top, axis=0)
    def summed(values):
        blocks = jnp.concatenate(
            [value.reshape(SIZE_H, value.shape[0] // SIZE_H, 128) for value in values], axis=1
        )
        blocks = (weight * blocks).reshape(SIZE_H, SIZE_X, blocks.shape[1] // SIZE_X, 128)
        return jnp.sum(lax.all_to_all(jnp.moveaxis(blocks, 1, 0), "pole", 0, 0), axis=0)

    def in_place(blocks):
        got = []
        for flip in range(2):
            piece = lax.dynamic_index_in_dim(blocks, core ^ flip, 0, keepdims=False)
            got.append(
                lax.ppermute(piece, LANE, lane_pairs(lambda h, l, c: (c ^ flip, l, h)))
            )
        return jnp.stack(in_order(zh, got[0], got[1]), axis=0)

    def everywhere(pair):
        every = jnp.moveaxis(spread(pair, "pole", SIZE_X), 0, 1)
        return every.reshape(pair.shape[0], SIZE_X * pair.shape[1], 128)

    diag_pieces = [top_diag]
    for step in range(3):
        diag_pieces += onward(diag_pieces, step)
    early = summed([outer, leaf_root[0], leaf_root[1], top_diag])
    diag_pieces[5], diag_pieces[6], early = lax.optimization_barrier(
        (diag_pieces[5], diag_pieces[6], early)
    )
    diag_pieces += onward(diag_pieces, 3)
    early = in_place(early)
    diag_pieces[7], diag_pieces[8], early = lax.optimization_barrier(
        (diag_pieces[7], diag_pieces[8], early)
    )
    (leaf_parent,) = with_copies(
        parent_kernel,
        [(2, 256, 128)],
        order,
        leaf_cols,
        cross_leaf,
        *diag_pieces,
        terms=256 * 1024 * 256,
    )
    late = summed([leaf_parent[0], leaf_parent[1]])
    early, late = lax.optimization_barrier((early, late))
    early = everywhere(early)

    cross = leaf_cross(core.reshape(1), pole_weights, leaf_parent, leaf_root, panels)
    cross, early = lax.optimization_barrier((cross, early))
    cross = cross.reshape(SIZE_X * SIZE_Y, 2, 2, 32, 128)
    cross = jnp.sum(lax.all_to_all(cross, ("pole", "y"), 0, 0), axis=0)
    late = in_place(late)
    got = []
    for flip in range(2):
        piece = lax.dynamic_index_in_dim(cross, core ^ flip, 0, keepdims=False)
        got.append(lax.ppermute(piece, PLANE, plane_pairs(flip)))
    cross = jnp.concatenate(in_order(core, got[0], got[1]), axis=0)
    ends = everywhere(jnp.concatenate([late.reshape(4, 32, 128), leaf - cross], axis=0))
    outer_dens = early[:, :256]
    rootward_dens = early[:, 256:768].reshape(4, 256, 128)
    top_dens = early[:, 768:]
    leaf_dens = ends[4:]
    parent_dens = jnp.moveaxis(ends[:4].reshape(2, 2, SIZE_X, 32, 128), 2, 1)
    parent_dens = parent_dens.reshape(4, 128, 128)
    return (top_dens, outer_dens, leaf_dens, parent_dens, rootward_dens)


def solution(mesh):
    fine = Mesh(
        mesh.devices.reshape(SIZE_X, SIZE_Y, SIZE_H, SIZE_L, SIZE_C),
        ("pole", "y", "zh", "zl", "core"),
    )
    row, col = ("y", "zh"), ("zl", "core")
    return jax.shard_map(
        body,
        mesh=fine,
        in_specs=(
            P("pole", row, col),
            P("pole", None, row, col),
            P("pole", None, row, col),
            P("pole", None, row, col),
            P("pole", None, row, col),
            P("pole", None, row, col),
            P(None, row),
            P(None, row),
            P(None, row),
            P("pole"),
        ),
        out_specs=(
            P(None, row, col),
            P(None, row, col),
            P(None, row, col),
            P(None, row, col),
            P(None, row, col),
        ),
        check_vma=False,
    )
```

```python
import math

import jax
import jax.numpy as jnp
from jax import lax
from jax.experimental import pallas as pl
from jax.experimental.pallas import tpu as pltpu
from jax.sharding import Mesh
from jax.sharding import PartitionSpec as P

RING = ("zh", "zl")
LANE = ("zh", "zl", "core")
PLANE = ("y", "zh", "zl", "core")
SIZE_X, SIZE_Y, SIZE_H, SIZE_L, SIZE_C = 4, 4, 2, 4, 2
SIZE_Z = SIZE_H * SIZE_L
VMEM = pltpu.CompilerParams(vmem_limit_bytes=64 * 1024 * 1024)
IN_VMEM = pl.BlockSpec(memory_space=pltpu.VMEM)
IN_SMEM = pl.BlockSpec(memory_space=pltpu.SMEM)


def block_mask(pattern, rows):
    width = rows // pattern.shape[-1]
    return jnp.repeat(pattern.astype(jnp.float32), width, axis=-1)


def lane_pairs(target):
    pairs = []
    for zh in range(SIZE_H):
        for zl in range(SIZE_L):
            for core in range(SIZE_C):
                to_h, to_l, to_c = target(zh, zl, core)
                pairs.append(
                    ((zh * SIZE_L + zl) * SIZE_C + core, (to_h * SIZE_L + to_l) * SIZE_C + to_c)
                )
    return pairs


def plane_pairs(flip):
    pairs = []
    for y in range(SIZE_Y):
        for zh in range(SIZE_H):
            for zl in range(SIZE_L):
                for core in range(SIZE_C):
                    here = ((y * SIZE_H + zh) * SIZE_L + zl) * SIZE_C + core
                    there = ((zl * SIZE_H + zh) * SIZE_L + y) * SIZE_C + (core ^ flip)
                    pairs.append((here, there))
    return pairs


def ring_pairs(step):
    return [(z, (z + step) % SIZE_Z) for z in range(SIZE_Z)]


def onward(pieces, step):
    ahead, behind = (pieces[-2], pieces[-1]) if step else (pieces[0], pieces[0])
    if step == 3:
        half = ahead.shape[0] // 2
        ahead, behind = ahead[:half], behind[half:]
    return [
        lax.ppermute(ahead, RING, ring_pairs(1)),
        lax.ppermute(behind, RING, ring_pairs(-1)),
    ]


def column_of(place):
    return (place % SIZE_L) * SIZE_H + place // SIZE_L


def spread(value, axis, size):
    return lax.all_to_all(jnp.broadcast_to(value[None], (size,) + value.shape), axis, 0, 0)


def in_order(flag, first, second):
    return jnp.where(flag == 0, first, second), jnp.where(flag == 0, second, first)


def split(value):
    high = value.astype(jnp.bfloat16)
    return high, (value - high.astype(jnp.float32)).astype(jnp.bfloat16)


def product(left, right, dims=((1,), (0,))):
    def one(a, b):
        return lax.dot_general(a, b, (dims, ((), ())), preferred_element_type=jnp.float32)

    return one(left[0], right[0]) + (one(left[0], right[1]) + one(left[1], right[0]))


def product_t(left, right):
    return product(left, right, ((0,), (0,)))


def fetched(sources, scratch, sems):
    copies = [
        pltpu.make_async_copy(source, to, sems.at[at])
        for at, (source, to) in enumerate(zip(sources, scratch))
    ]
    for copy in copies:
        copy.start()

    def ready(at):
        copies[at].wait()
        return scratch[at]

    return ready


def outer_kernel(inverse, top, out, inverse_here, top_here, sems):
    order = [half * 8 + k for k in range(8) for half in range(2)]
    ready = fetched(
        [top] + [inverse.at[at] for at in order],
        [top_here] + [inverse_here.at[at] for at in order],
        sems,
    )
    ready(0)
    totals = [None, None]
    for k in range(8):
        right = split(top_here[k])
        for half in range(2):
            left = split(ready(1 + k * 2 + half)[...])
            part = product(left, right)
            totals[half] = part if k == 0 else totals[half] + part
    for half in range(2):
        out[half * 256 : (half + 1) * 256, :] = -totals[half]


def cross_kernel(order, *refs):
    sources, (top_out, leaf_out) = refs[:11], refs[11:13]
    scratch, sems = refs[13:24], refs[24]
    ready = fetched(sources, scratch, sems)
    top, mine = ready(0), ready(1)
    panels = split(
        jnp.concatenate(
            [
                jnp.concatenate([top[zh], mine[zh, 256:512, :], mine[zh, 512:768, :]], axis=1)
                for zh in range(SIZE_H)
            ],
            axis=0,
        )
    )
    for at in range(8):
        if at < 7:
            piece = ready(2 + at)[...]
        else:
            piece = jnp.concatenate([ready(9)[...], ready(10)[...]], axis=0)
        part = product_t(split(piece), panels)
        top_out[order[at]] = part[:, :128]
        leaf_out[order[at], 0] = part[:, 128:256]
        leaf_out[order[at], 1] = part[:, 256:]


def root_kernel(order, *refs):
    sources, out = refs[:11], refs[11]
    scratch, sems = refs[12:23], refs[23]
    ready = fetched(sources, scratch, sems)
    cols, inverse = ready(0), ready(1)
    totals = [jnp.zeros((256, 256), jnp.float32) for _ in range(2)]
    for k in range(8):
        root = split(jnp.concatenate([cols[k, 256:512, :], cols[k, 512:768, :]], axis=1))
        for half in range(2):
            totals[half] += product(split(inverse[half * 8 + k]), root)
    for at in range(8):
        if at < 7:
            piece = ready(2 + at)[...]
        else:
            piece = jnp.concatenate([ready(9)[...], ready(10)[...]], axis=0)
        place = order[at]
        parent = split(
            jnp.concatenate([cols[place, 0:128, :], cols[place, 128:256, :]], axis=1)
        )
        for half in range(2):
            totals[half] += product(split(piece[half * 256 : (half + 1) * 256]), parent)
    for half in range(2):
        for leaf in range(2):
            out[leaf, half * 256 : (half + 1) * 256, :] = -totals[half][
                :, leaf * 128 : (leaf + 1) * 128
            ]


def parent_kernel(order, *refs):
    sources, out, scratch, sems = refs[:11], refs[11], refs[12:23], refs[23]
    ready = fetched(sources, scratch, sems)
    cols, cross = ready(0), ready(1)
    total = jnp.zeros((256, 256), jnp.float32)
    for at in range(8):
        if at < 7:
            piece = ready(2 + at)[...]
        else:
            piece = jnp.concatenate([ready(9)[...], ready(10)[...]], axis=0)
        place = order[at]
        parent = jnp.concatenate([cols[place, 0:128, :], cols[place, 128:256, :]], axis=1)
        total += product(split(piece), split(parent))
    for leaf in range(2):
        for sub in range(2):
            added = cross[0, sub, leaf]
            for y in range(1, SIZE_Y):
                added += cross[y, sub, leaf]
            rows = slice(sub * 128, (sub + 1) * 128)
            out[leaf, rows, :] = -(total[rows, leaf * 128 : (leaf + 1) * 128] + added)


def leaf_kernel(core, weight, parent, root, panels, out, high, low):
    @pl.when(pl.program_id(0) == 0)
    def _():
        for leaf in range(2):
            rows = jnp.concatenate(
                [
                    parent[leaf, 0:128, :],
                    root[leaf, 0:256, :],
                    parent[leaf, 128:256, :],
                    root[leaf, 256:512, :],
                ],
                axis=0,
            )
            high[leaf], low[leaf] = split(jnp.transpose(rows))

    for leaf in range(2):
        right = jnp.concatenate(
            [
                jnp.concatenate([panels[half, 0, 0, leaf], panels[half, 0, 1, leaf]], axis=1)
                for half in range(SIZE_H)
            ],
            axis=0,
        )
        done = weight[0] * product((high[leaf], low[leaf]), split(right))
        for side in range(2):
            out[:, 0, side, leaf] = done[:, side * 128 : (side + 1) * 128].reshape(
                SIZE_X, 32, 128
            )


def leaf_cross(core, weight, parent, root, panels):
    panels = panels.reshape(SIZE_H, SIZE_L, SIZE_C, 4, 384, 128)
    return pl.pallas_call(
        leaf_kernel,
        out_shape=jax.ShapeDtypeStruct((SIZE_X, SIZE_Y, 2, 2, 32, 128), jnp.float32),
        grid_spec=pltpu.PrefetchScalarGridSpec(
            num_scalar_prefetch=1,
            grid=(SIZE_L,),
            in_specs=[
                IN_SMEM,
                pl.BlockSpec((2, 256, 128), lambda l, core: (0, 0, 0)),
                pl.BlockSpec((2, 512, 128), lambda l, core: (0, 0, 0)),
                pl.BlockSpec(
                    (SIZE_H, 1, SIZE_C, 2, 384, 128), lambda l, core: (0, l, 0, core[0], 0, 0)
                ),
            ],
            out_specs=pl.BlockSpec(
                (SIZE_X, 1, 2, 2, 32, 128), lambda l, core: (0, l, 0, 0, 0, 0)
            ),
            scratch_shapes=[
                pltpu.VMEM((2, 128, 768), jnp.bfloat16),
                pltpu.VMEM((2, 128, 768), jnp.bfloat16),
            ],
        ),
        cost_estimate=cost(2 * 768 * 1024 * 128, [(2, 768, 1024), (2, 768, 128), (2, 1024, 128)]),
        compiler_params=VMEM,
    )(core, weight, parent, root, panels)


def cost(terms, arrays):
    moved = 4 * sum(math.prod(shape) for shape in arrays)
    return pl.CostEstimate(flops=6 * terms, bytes_accessed=moved, transcendentals=0)


def with_copies(kernel, shapes, order, *operands, terms, copies=None):
    specs = [pl.BlockSpec(memory_space=pl.ANY)] * len(operands)
    scratch = [pltpu.VMEM(operand.shape, jnp.float32) for operand in operands]
    scratch.append(pltpu.SemaphoreType.DMA((copies or len(operands),)))
    price = cost(terms, [operand.shape for operand in operands] + shapes)
    if order is not None:
        specs, operands = [IN_SMEM] + specs, (order,) + operands
    return pl.pallas_call(
        kernel,
        out_shape=[jax.ShapeDtypeStruct(shape, jnp.float32) for shape in shapes],
        in_specs=specs,
        out_specs=[IN_VMEM] * len(shapes),
        scratch_shapes=scratch,
        cost_estimate=price,
        compiler_params=VMEM,
    )(*operands)


def body(
    root_inverse,
    top_factor,
    parent_factor,
    root_factor,
    top_pivots_inv,
    leaf_pivots_inv,
    pattern_top,
    pattern_parent,
    pattern_root,
    pole_weights,
):
    zh = lax.axis_index("zh")
    zl = lax.axis_index("zl")
    core = lax.axis_index("core")
    place = zh * SIZE_L + zl
    weight = pole_weights[0]

    top = top_factor[0] * block_mask(pattern_top, 256)[:, :, None]
    parent = parent_factor[0] * block_mask(pattern_parent, 128)[:, :, None]
    root = root_factor[0] * block_mask(pattern_root, 256)[:, :, None]

    leaves = jnp.concatenate([parent, root], axis=1)

    def to_ring(value):
        got = []
        for flip in range(2):
            piece = lax.dynamic_index_in_dim(value, zh ^ flip, 0, keepdims=False)
            got.append(
                lax.ppermute(piece, LANE, lane_pairs(lambda h, l, c: (c, l, h ^ flip)))
            )
        return jnp.stack(in_order(core, got[0], got[1]))

    inverse = lax.all_gather(root_inverse[0], LANE, axis=0)

    top_block = to_ring(jnp.concatenate([top, top_pivots_inv[0]], axis=1))
    top_block, parent, root = lax.optimization_barrier((top_block, parent, root))
    leaf_block = to_ring(
        jnp.concatenate([parent.reshape(2, 256, 128), root.reshape(2, 512, 128)], axis=1)
    )
    pivot_block = top_block[:, 256:].reshape(256, 128)
    top_block = top_block[:, :256]
    top_cols = spread(top_block, "y", SIZE_Y).reshape(8, 256, 128)
    leaf = (weight * leaf_pivots_inv[0]).reshape(4, SIZE_X, 32, 128)
    leaf = jnp.sum(lax.all_to_all(jnp.moveaxis(leaf, 1, 0), "pole", 0, 0), axis=0)
    top_cols, leaf, leaf_block = lax.optimization_barrier((top_cols, leaf, leaf_block))
    inverse, leaf_block = lax.optimization_barrier((inverse, leaf_block))
    leaf_cols = lax.all_gather(leaf_block, "y", axis=0).reshape(8, 768, 128)

    (outer,) = with_copies(
        outer_kernel,
        [(512, 128)],
        None,
        inverse,
        top_cols,
        terms=512 * 2048 * 128,
        copies=17,
    )
    pieces = [outer]
    for step in range(3):
        pieces += onward(pieces, step)
    pieces += onward(pieces, 3)
    pieces[7], pieces[8], leaves = lax.optimization_barrier((pieces[7], pieces[8], leaves))
    panels = lax.all_gather(leaves, LANE, axis=0)
    order = jnp.stack([column_of((place + d) % SIZE_Z) for d in (0, 7, 1, 6, 2, 5, 3, 4)])

    cross_top, cross_leaf = with_copies(
        cross_kernel,
        [(8, 128, 128), (8, 2, 128, 128)],
        order,
        top_block,
        leaf_block,
        *pieces,
        terms=512 * 1024 * 384,
    )
    cross_leaf, leaf_cols = lax.optimization_barrier((cross_leaf, leaf_cols))
    (leaf_root,) = with_copies(
        root_kernel,
        [(2, 512, 128)],
        order,
        leaf_cols,
        inverse,
        *pieces,
        terms=512 * 3072 * 256,
    )
    cross_top = lax.all_to_all(cross_top.reshape(SIZE_Y, 256, 128), "y", 0, 0)
    cross_top, cross_leaf, leaf_root = lax.optimization_barrier(
        (cross_top, cross_leaf, leaf_root)
    )
    cross_leaf = lax.all_to_all(cross_leaf.reshape(SIZE_Y, 2, 2, 128, 128), "y", 0, 0)
    top_diag = pivot_block - jnp.sum(cross_top, axis=0)
    def summed(values):
        blocks = jnp.concatenate(
            [value.reshape(SIZE_H, value.shape[0] // SIZE_H, 128) for value in values], axis=1
        )
        blocks = (weight * blocks).reshape(SIZE_H, SIZE_X, blocks.shape[1] // SIZE_X, 128)
        return jnp.sum(lax.all_to_all(jnp.moveaxis(blocks, 1, 0), "pole", 0, 0), axis=0)

    def in_place(blocks):
        got = []
        for flip in range(2):
            piece = lax.dynamic_index_in_dim(blocks, core ^ flip, 0, keepdims=False)
            got.append(
                lax.ppermute(piece, LANE, lane_pairs(lambda h, l, c: (c ^ flip, l, h)))
            )
        return jnp.stack(in_order(zh, got[0], got[1]), axis=0)

    def everywhere(pair):
        every = jnp.moveaxis(spread(pair, "pole", SIZE_X), 0, 1)
        return every.reshape(pair.shape[0], SIZE_X * pair.shape[1], 128)

    diag_pieces = [top_diag]
    for step in range(3):
        diag_pieces += onward(diag_pieces, step)
    early = summed([outer, leaf_root[0], leaf_root[1], top_diag])
    diag_pieces[5], diag_pieces[6], early = lax.optimization_barrier(
        (diag_pieces[5], diag_pieces[6], early)
    )
    diag_pieces += onward(diag_pieces, 3)
    early = in_place(early)
    diag_pieces[7], diag_pieces[8], early = lax.optimization_barrier(
        (diag_pieces[7], diag_pieces[8], early)
    )
    (leaf_parent,) = with_copies(
        parent_kernel,
        [(2, 256, 128)],
        order,
        leaf_cols,
        cross_leaf,
        *diag_pieces,
        terms=256 * 1024 * 256,
    )
    early = everywhere(early)
    late = summed([leaf_parent[0], leaf_parent[1]])

    cross = leaf_cross(core.reshape(1), pole_weights, leaf_parent, leaf_root, panels)
    cross, early = lax.optimization_barrier((cross, early))
    cross = cross.reshape(SIZE_X * SIZE_Y, 2, 2, 32, 128)
    cross = jnp.sum(lax.all_to_all(cross, ("pole", "y"), 0, 0), axis=0)
    late = in_place(late)
    got = []
    for flip in range(2):
        piece = lax.dynamic_index_in_dim(cross, core ^ flip, 0, keepdims=False)
        got.append(lax.ppermute(piece, PLANE, plane_pairs(flip)))
    cross = jnp.concatenate(in_order(core, got[0], got[1]), axis=0)
    ends = everywhere(jnp.concatenate([late.reshape(4, 32, 128), leaf - cross], axis=0))
    outer_dens = early[:, :256]
    rootward_dens = early[:, 256:768].reshape(4, 256, 128)
    top_dens = early[:, 768:]
    leaf_dens = ends[4:]
    parent_dens = jnp.moveaxis(ends[:4].reshape(2, 2, SIZE_X, 32, 128), 2, 1)
    parent_dens = parent_dens.reshape(4, 128, 128)
    return (top_dens, outer_dens, leaf_dens, parent_dens, rootward_dens)


def solution(mesh):
    fine = Mesh(
        mesh.devices.reshape(SIZE_X, SIZE_Y, SIZE_H, SIZE_L, SIZE_C),
        ("pole", "y", "zh", "zl", "core"),
    )
    row, col = ("y", "zh"), ("zl", "core")
    return jax.shard_map(
        body,
        mesh=fine,
        in_specs=(
            P("pole", row, col),
            P("pole", None, row, col),
            P("pole", None, row, col),
            P("pole", None, row, col),
            P("pole", None, row, col),
            P("pole", None, row, col),
            P(None, row),
            P(None, row),
            P(None, row),
            P("pole"),
        ),
        out_specs=(
            P(None, row, col),
            P(None, row, col),
            P(None, row, col),
            P(None, row, col),
            P(None, row, col),
        ),
        check_vma=False,
    )
```
